32 devices in a mesh: rot: 8 (over z, y), fft: 4 (over x, core).
Axes of the slice: x: 2, y: 2, z: 4, core: 2. Of those that a mesh axis runs over, the one named last changes fastest.
Arguments:
- receptor: bfloat16 [2, 11, 128, 128, 128], P(None, None, 'fft'), may hold values from -6 to 6, as said below
- ligand_grids: bfloat16 [32, 11, 32, 1024], P(None, None, 'fft'), may hold values from -8 to 8
- rot_index: int32 [48], P('rot'), parts along dimension 0, may hold values from 0 to 31
Outputs:
- scores: float32 [48, 128, 128, 128], P('rot', 'fft'), parts along dimension 0
- best: float32 [48], P('rot'), parts along dimension 0
The draws below stay inside these ranges and needn't reach their ends.
There are 8 independent parts, one for each index of `rot`. The reference program is written for one: setup_inputs(seed, part) draws one part's arguments, and reference() takes and returns one part's arrays. A program takes and returns all parts, laid end to end along the dimension named above; an argument that names none is the same for every part. Nothing has to cross between parts.
Inputs may be any that keep to these rules, and one draw needn't show every extreme that they name: The receptor spectra are those of real grids: in every channel the entry at frequency (-kz, -kx, -ky), taken modulo 128 along each dimension, is the complex conjugate of the entry at (kz, kx, ky).
All inputs are finite; a program needn't handle non-finite values.
Results may differ from the reference program's by a relative error of at most 0.0003.
Values may be sent and summed in bfloat16 or wider, within the bound.
A program may use at most 256 MiB of HBM per device.

```python
import jax
import jax.numpy as jnp
from jax import lax

N = 128
CH = 11
LB = 32
ROT_SET = 32
ROTS = 6


def draw_receptor(key, part):
    first_key = jax.random.fold_in(key, 0)
    grid_shape = (2, CH, N, N, N)
    sample = jnp.clip(jax.random.normal(first_key, grid_shape, jnp.float32), -4.0, 4.0)
    mirror = jnp.roll(jnp.flip(sample, axis=(2, 3, 4)), 1, axis=(2, 3, 4))
    real_part = (sample[0] + mirror[0]) * 0.5 ** 0.5
    imag_part = (sample[1] - mirror[1]) * 0.5 ** 0.5
    return jnp.stack([real_part, imag_part]).astype(jnp.bfloat16)


def plant(array, own_key, least, largest):
    longest = array.shape.index(max(array.shape))
    spots = []
    for shift in (0, 1):
        where = [jax.random.randint(jax.random.fold_in(own_key, axis), (), 0, length) for axis, length in enumerate(array.shape)]
        where[longest] = (where[longest] + shift) % array.shape[longest]
        spots.append(tuple(where))
    return array.at[spots[0]].set(least).at[spots[1]].set(largest)


def block_levels(key, dims, cuts, least, top_value):
    def one(dim, shards_of):
        heights = jax.random.uniform(jax.random.fold_in(jax.random.fold_in(key, 6), dim), (shards_of,), jnp.float32, least / len(cuts), top_value / len(cuts))
        return jnp.repeat(jnp.exp(heights), dims[dim] // shards_of).reshape((-1,) + (1,) * (len(dims) - dim - 1))

    loudness = one(*cuts[0])
    for cut in cuts[1:]:
        loudness = loudness * one(*cut)
    return loudness


def noise(own_key, extent, scale, most, shards=(), kind=jnp.bfloat16):
    level = block_levels(own_key, extent, shards, -0.22, 0.18) if shards else 1.0
    array = jax.random.normal(own_key, extent, jnp.float32) * scale * level
    return jnp.minimum(jnp.maximum(array, -most), most).astype(kind)


def setup_inputs(seed: int = 0, part: int = 0) -> dict:
    splits = jax.random.split(jax.random.key(seed), 4)
    part_keys = jax.random.split(jax.random.fold_in(splits[3], part), 4)
    return {
        "receptor": draw_receptor(jax.random.fold_in(splits[3], 71), part),
        "ligand_grids": noise(splits[1], (ROT_SET, CH, LB, LB * LB), 2.0, 8.0, ((2, 4),)),
        "rot_index": plant(jax.random.randint(part_keys[2], (ROTS,), 0, ROT_SET), jax.random.fold_in(part_keys[2], 1), 0, ROT_SET - 1).astype(jnp.int32),
    }


def reference(receptor, ligand_grids, rot_index):
    spectra = lax.complex(receptor[0].astype(jnp.float32), receptor[1].astype(jnp.float32))

    def one_rotation(which):
        grid = ligand_grids[which].astype(jnp.float32).reshape(CH, LB, LB, LB)
        padded = jnp.zeros((CH, N, N, N), jnp.float32).at[:, :LB, :LB, :LB].set(grid)
        ligand_spectrum = jnp.fft.fftn(padded, axes=(1, 2, 3))
        product = jnp.sum(spectra * jnp.conj(ligand_spectrum), axis=0)
        field = jnp.real(jnp.fft.ifftn(product))
        return jnp.transpose(field, (1, 2, 0))

    scores = lax.map(one_rotation, rot_index)
    best = jnp.min(scores, axis=(1, 2, 3))
    return scores, best
```

```python
import functools
import math

import jax
import jax.numpy as jnp
import ml_dtypes
import numpy as np
from jax import lax
from jax.experimental import pallas as pl
from jax.experimental.pallas import tpu as pltpu
from jax.sharding import PartitionSpec as P

BF = jnp.bfloat16
F32 = jnp.float32
TOP = 32767.0
LEVELS = 256.0


def halves(table):
    upper = table.astype(np.float32).astype(ml_dtypes.bfloat16)
    lower = (table - upper.astype(np.float64)).astype(np.float32)
    return upper, lower.astype(ml_dtypes.bfloat16)


def trig(rows, cols, length):
    angle = (np.outer(rows, cols) % length) * (2.0 * math.pi / length)
    return np.cos(angle), np.sin(angle)


def split(values):
    upper = values.astype(BF)
    return upper, (values - upper.astype(F32)).astype(BF)


def mul(left, right):
    return jnp.dot(left, right, preferred_element_type=F32)


def mul_t(left, right):
    return lax.dot_general(left, right, (((1,), (1,)), ((), ())), preferred_element_type=F32)


def up(value, step):
    return -(-value // step) * step


def pick_kernel(channels, block, index_ref, in_ref, out_ref):
    depth = in_ref.shape[2]
    parts = [in_ref[0, c].astype(F32) for c in range(channels)]
    if block > channels * depth:
        parts.append(jnp.zeros((block - channels * depth, in_ref.shape[3]), F32))
    out_ref[0] = jnp.concatenate(parts, axis=0).astype(BF)


def main_kernel(
    channels, planes, box, groups, rotations, length, block, rows,
    rec_hbm, own_hbm, tz_hbm, wy_ref, tx_ref, ti_ref, recv_hbm,
    rec, lbuf, tz, a_buf, b_re, b_im, qbuf,
    load_sem, own_sem, gsend, grecv, xsend, xrecv, self_sem,
):
    me = lax.axis_index("fft")
    xs = length // groups
    sib = me + 1 - 2 * lax.rem(me, 2)
    far = [lax.rem(me + 2 * m, groups) for m in range(1, groups // 2)]
    peers = [sib] + far
    others = [lax.rem(me + s, groups) for s in range(1, groups)]
    half = length // 2

    rec_copy = pltpu.make_async_copy(rec_hbm.at[:, :, pl.ds(0, planes)], rec, load_sem.at[0])
    rec_copy.start()
    tz_copy = pltpu.make_async_copy(tz_hbm.at[me], tz, load_sem.at[1])
    tz_copy.start()

    barrier = pltpu.get_barrier_semaphore()
    for peer in others:
        pl.semaphore_signal(barrier, inc=1, device_id={"fft": peer}, device_id_type=pl.DeviceIdType.MESH)
    pl.semaphore_wait(barrier, groups - 1)

    def slot(r, source):
        return lbuf.at[r, pl.ds(pl.multiple_of(source * block, block), block)]

    def own_copy(r, k):
        return pltpu.make_async_remote_copy(
            src_ref=own_hbm.at[r], dst_ref=slot(r, me), send_sem=gsend.at[r, k], recv_sem=grecv.at[r, me],
            device_id={"fft": peers[k]}, device_id_type=pl.DeviceIdType.MESH)

    def relay_copy(r, k):
        return pltpu.make_async_remote_copy(
            src_ref=slot(r, far[k]), dst_ref=slot(r, far[k]), send_sem=gsend.at[r, len(peers) + k],
            recv_sem=grecv.at[r, far[k]], device_id={"fft": sib}, device_id_type=pl.DeviceIdType.MESH)

    def arrival(r, source):
        return pltpu.make_async_remote_copy(
            src_ref=own_hbm.at[r], dst_ref=slot(r, source), send_sem=gsend.at[r, 0], recv_sem=grecv.at[r, source],
            device_id={"fft": sib}, device_id_type=pl.DeviceIdType.MESH)

    def local(r):
        return pltpu.make_async_copy(own_hbm.at[r], slot(r, me), own_sem.at[r])

    def begin(r):
        for k in range(len(peers)):
            own_copy(r, k).start()
        local(r).start()

    def relay(r):
        for k in range(len(far)):
            arrival(r, far[k]).wait_recv()
            relay_copy(r, k).start()

    def finish(r):
        arrival(r, sib).wait_recv()
        for m in range(1, groups // 2):
            arrival(r, lax.rem(sib + 2 * m, groups)).wait_recv()
        local(r).wait()

    def send_plane(r, k, s):
        peer = others[s]
        return pltpu.make_async_remote_copy(
            src_ref=qbuf.at[r, k, peer], dst_ref=recv_hbm.at[r, me, k],
            send_sem=xsend.at[r, s], recv_sem=xrecv.at[r, me],
            device_id={"fft": peer}, device_id_type=pl.DeviceIdType.MESH)

    def send_all(r, s):
        peer = others[s]
        return pltpu.make_async_remote_copy(
            src_ref=qbuf.at[r, :, peer], dst_ref=recv_hbm.at[r, peer],
            send_sem=xsend.at[r, s], recv_sem=xrecv.at[r, peer],
            device_id={"fft": peer}, device_id_type=pl.DeviceIdType.MESH)

    def keep(r):
        return pltpu.make_async_copy(
            qbuf.at[r, :, me], recv_hbm.at[r, me], self_sem.at[r])

    lanes = lax.broadcasted_iota(jnp.int32, (length, length), 1)

    def forward(r):
        finish(r)
        cells = lbuf[r]
        a_buf[...] = mul(tz[0], cells) + mul(tz[1], cells)

        @pl.when(r + 1 < rotations)
        def _():
            relay(r + 1)

        @pl.when(r + 2 < rotations)
        def _():
            begin(r + 2)

        def lane_group(j, carry):
            at = pl.ds(pl.multiple_of(j * 128, 128), 128)
            upper, lower = split(jnp.concatenate([a_buf[0:rows, at], a_buf[rows : 2 * rows, at]], axis=1))
            both = jnp.concatenate([upper, lower, upper], axis=1)
            per = 128 // box
            for i in range(per):
                out = mul(both, wy_ref[i])
                b_re[pl.ds(j * per + i, rows, stride=box), :] = out[:, :length]
                b_im[pl.ds(j * per + i, rows, stride=box), :] = out[:, length:]
            return carry

        lax.fori_loop(0, box * box // 128, lane_group, 0)

        @pl.when(r == 0)
        def _():
            rec_copy.wait()

        def plane(k, expo):
            p_re = p_im = None
            for c0 in range(0, channels, 2):
                pair = range(c0, min(c0 + 2, channels))
                at = [pl.ds(pl.multiple_of((k * channels + c) * box, box), box) for c in pair]
                re_hi, re_lo = split(jnp.concatenate([b_re[a, :] for a in at], axis=1))
                im_hi, im_lo = split(jnp.concatenate([b_im[a, :] for a in at], axis=1))
                spec = mul(tx_ref[...], jnp.concatenate([re_hi, im_hi, re_lo, im_lo, re_hi, im_hi], axis=0))
                for t, c in enumerate(pair):
                    s_re = spec[:length, t * length : (t + 1) * length]
                    s_im = spec[length:, t * length : (t + 1) * length]
                    r_re = rec[0, c, k].astype(F32)
                    r_im = rec[1, c, k].astype(F32)
                    q_re = r_re * s_re + r_im * s_im
                    q_im = r_im * s_re - r_re * s_im
                    p_re = q_re if p_re is None else p_re + q_re
                    p_im = q_im if p_im is None else p_im + q_im
            re_hi, re_lo = split(p_re)
            im_hi, im_lo = split(p_im)
            def square(re, im):
                return jnp.concatenate(
                    [jnp.concatenate([re, im], axis=1), jnp.concatenate([-im, re], axis=1)], axis=0)
            first = mul(ti_ref[...], square(re_hi, im_hi))
            field = first[:length] + first[length:] + mul(ti_ref[0:length], square(re_lo, im_lo))
            most = jnp.max(jnp.abs(field), axis=1, keepdims=True)
            code = jnp.ceil(LEVELS * jnp.log2(jnp.maximum(most, 1e-30))) + 1.0
            factor = TOP * jnp.exp2(code * (-1.0 / LEVELS))
            qbuf[r, k] = jnp.round(field * factor).astype(jnp.int32).reshape(groups, xs, 2 * length).astype(jnp.int16)
            for s in range(groups - 1):
                send_plane(r, k, s).start()
            return jnp.where(lanes == k, code, expo)

        expo = lax.fori_loop(0, planes, plane, jnp.zeros((length, length), F32))
        codes = jnp.concatenate([expo, expo], axis=1).astype(jnp.int32)
        qbuf[r, planes] = codes.reshape(groups, xs, 2 * length).astype(jnp.int16)
        for s in range(groups - 1):
            send_plane(r, planes, s).start()
        keep(r).start()

    begin(0)
    if rotations > 1:
        begin(1)
    tz_copy.wait()
    relay(0)

    def rotation(r, carry):
        forward(r)
        return carry

    lax.fori_loop(0, rotations, rotation, 0)

    def drain(r, carry):
        for k in range(len(peers)):
            own_copy(r, k).wait_send()
        for k in range(len(far)):
            relay_copy(r, k).wait_send()
        for s in range(groups - 1):
            send_all(r, s).wait_send()
            send_all(r, s).wait_recv()
        keep(r).wait()
        return carry

    lax.fori_loop(0, rotations, drain, 0)


def final_kernel(groups, planes, length, width, terms, blocks_ref, tz_ref, tw_ref, out_ref, low_ref, f_re, f_im):
    for s in range(groups):
        code = blocks_ref[0, s, planes].astype(jnp.int32).astype(F32)[:, :length]
        scale = jnp.exp2(code * (1.0 / LEVELS)) * (1.0 / TOP)
        for k in range(planes):
            value = blocks_ref[0, s, k].astype(jnp.int32).astype(F32) * scale[:, k : k + 1]
            at = pl.ds((s * planes + k) * width, width)
            f_re[at, :] = value[:, :length]
            f_im[at, :] = value[:, length:]
    if terms > groups * planes:
        rest = pl.ds(groups * planes * width, (terms - groups * planes) * width)
        f_re[rest, :] = jnp.zeros(((terms - groups * planes) * width, length), F32)
        f_im[rest, :] = jnp.zeros(((terms - groups * planes) * width, length), F32)
    for i in range(width):
        at = pl.ds(i, terms, stride=width)
        upper, lower = split(jnp.concatenate([f_re[at, :], f_im[at, :]], axis=1))
        both = mul(tz_ref[...], jnp.concatenate([upper, lower, upper], axis=0))
        g_re = both[:length, :length] - both[length:, length:]
        g_im = both[:length, length:] + both[length:, :length]
        upper, lower = split(jnp.concatenate([g_re, g_im], axis=1))
        first = mul_t(tw_ref[...], upper)
        plane = first[:length] + first[length:] + mul_t(tw_ref[0:length], lower)
        out_ref[0, i] = plane
        low_ref[0, 0, i : i + 1, :] = jnp.min(plane, axis=0, keepdims=True)


def shards(receptor, ligand_grids, rot_index):
    groups = lax.axis_size("fft")
    channels, slab, length = receptor.shape[1], receptor.shape[2], receptor.shape[3]
    depth = ligand_grids.shape[2]
    box = depth * groups
    cells = ligand_grids.shape[3]
    rotations = rot_index.shape[0]
    xs = length // groups
    planes = slab // 2 + 1
    block = up(channels * depth, 16)
    rows = up(planes * channels, 16)
    freq = np.arange(length)

    t_z = np.zeros((groups, 2, rows, groups, block))
    for d in range(groups):
        cz, sz = trig(d * slab + np.arange(planes), np.arange(box), length)
        for c in range(channels):
            at = np.arange(planes) * channels + c
            for s in range(groups):
                span = slice(c * depth, (c + 1) * depth)
                cut = slice(s * depth, (s + 1) * depth)
                t_z[d, 0, at, s, span] = cz[:, cut]
                t_z[d, 1, at, s, span] = -sz[:, cut]
    t_z = t_z.reshape(groups, 2 * rows, groups * block)
    t_z = jnp.asarray(np.stack(halves(t_z), axis=1))

    cy, sy = trig(np.arange(box), freq, length)
    per = 128 // box
    w_y = np.zeros((per, 256, 2 * length))
    for i in range(per):
        w_y[i, i * box : (i + 1) * box] = np.concatenate([cy, -sy], axis=1)
        w_y[i, 128 + i * box : 128 + (i + 1) * box] = np.concatenate([sy, cy], axis=1)
    hi, lo = halves(w_y)
    w_y = jnp.asarray(np.concatenate([hi, hi, lo], axis=1))

    t_x = np.block([[cy.T, sy.T], [-sy.T, cy.T]])
    hi, lo = halves(t_x)
    t_x = jnp.asarray(np.concatenate([hi, hi, lo], axis=1))

    cf, sf = trig(freq, freq, length)
    t_i = jnp.asarray(np.concatenate(halves(np.concatenate([cf, sf], axis=1)), axis=0))

    terms = up(groups * planes, 16)
    kz = np.zeros(terms, np.int64)
    weight = np.zeros(terms)
    for d in range(groups):
        for k in range(planes):
            f = d * slab + k
            kz[d * planes + k] = f
            if d < groups // 2:
                used = k < slab // 2
            else:
                used = k > 0 or f == length // 2
            weight[d * planes + k] = 0.0 if not used else 1.0 if f in (0, length // 2) else 2.0
    cb, sb = trig(freq, kz, length)
    hi, lo = halves(np.concatenate([cb * weight, sb * weight], axis=0))
    t_b = jnp.asarray(np.concatenate([hi, hi, lo], axis=1))
    t_w = jnp.asarray(np.concatenate(halves(np.concatenate([cf, -sf], axis=1) / float(length) ** 3), axis=0))

    own = pl.pallas_call(
        functools.partial(pick_kernel, channels, block),
        grid_spec=pltpu.PrefetchScalarGridSpec(
            num_scalar_prefetch=1,
            grid=(rotations,),
            in_specs=[pl.BlockSpec((1, channels, depth, cells), lambda r, index: (index[r], 0, 0, 0))],
            out_specs=pl.BlockSpec((1, block, cells), lambda r, index: (r, 0, 0)),
        ),
        out_shape=jax.ShapeDtypeStruct((rotations, block, cells), BF),
    )(rot_index, ligand_grids)

    any_space = pl.BlockSpec(memory_space=pl.ANY)
    vmem = pl.BlockSpec(memory_space=pltpu.VMEM)
    sent = pl.pallas_call(
        functools.partial(main_kernel, channels, planes, box, groups, rotations, length, block, rows),
        in_specs=[any_space, any_space, any_space, vmem, vmem, vmem],
        out_specs=any_space,
        out_shape=jax.ShapeDtypeStruct((rotations, groups, planes + 1, xs, 2 * length), jnp.int16),
        scratch_shapes=[
            pltpu.VMEM((2, channels, planes, length, length), BF),
            pltpu.VMEM((rotations, groups * block, cells), BF),
            pltpu.VMEM((2, 2 * rows, groups * block), BF),
            pltpu.VMEM((2 * rows, cells), F32),
            pltpu.VMEM((rows * box, length), F32),
            pltpu.VMEM((rows * box, length), F32),
            pltpu.VMEM((rotations, planes + 1, groups, xs, 2 * length), jnp.int16),
            pltpu.SemaphoreType.DMA((2,)),
            pltpu.SemaphoreType.DMA((rotations,)),
            pltpu.SemaphoreType.DMA((rotations, groups)),
            pltpu.SemaphoreType.DMA((rotations, groups)),
            pltpu.SemaphoreType.DMA((rotations, groups)),
            pltpu.SemaphoreType.DMA((rotations, groups)),
            pltpu.SemaphoreType.DMA((rotations,)),
        ],
        compiler_params=pltpu.CompilerParams(
            collective_id=0, has_side_effects=True, vmem_limit_bytes=56 * 2**20),
        cost_estimate=pl.CostEstimate(flops=rotations * 6 * 10**9, bytes_accessed=30_000_000, transcendentals=0),
    )(receptor, own, t_z, w_y, t_x, t_i)

    width = min(16, xs)
    scores, lows = pl.pallas_call(
        functools.partial(final_kernel, groups, planes, length, width, terms),
        grid=(rotations, xs // width),
        in_specs=[
            pl.BlockSpec((1, groups, planes + 1, width, 2 * length), lambda r, x: (r, 0, 0, x, 0)),
            pl.BlockSpec(t_b.shape, lambda r, x: (0, 0)),
            pl.BlockSpec(t_w.shape, lambda r, x: (0, 0)),
        ],
        out_specs=[
            pl.BlockSpec((1, width, length, length), lambda r, x: (r, x, 0, 0)),
            pl.BlockSpec((1, 1, width, length), lambda r, x: (r, x, 0, 0)),
        ],
        out_shape=[
            jax.ShapeDtypeStruct((rotations, xs, length, length), F32),
            jax.ShapeDtypeStruct((rotations, xs // width, width, length), F32),
        ],
        scratch_shapes=[pltpu.VMEM((terms * width, length), F32)] * 2,
        compiler_params=pltpu.CompilerParams(vmem_limit_bytes=32 * 2**20),
        cost_estimate=pl.CostEstimate(flops=rotations * 10**9, bytes_accessed=20_000_000, transcendentals=0),
    )(sent, t_b, t_w)
    best = lax.pmin(jnp.min(lows, axis=(1, 2, 3)), "fft")
    return scores, best


def solution(mesh):
    placed = (P(None, None, "fft", None, None), P(None, None, "fft", None), P("rot"))
    return jax.shard_map(
        shards,
        mesh=mesh,
        in_specs=placed,
        out_specs=(P("rot", "fft", None, None), P("rot")),
        check_vma=False,
    )
```

```python
import functools
import math

import jax
import jax.numpy as jnp
import ml_dtypes
import numpy as np
from jax import lax
from jax.experimental import pallas as pl
from jax.experimental.pallas import tpu as pltpu
from jax.sharding import PartitionSpec as P

BF = jnp.bfloat16
F32 = jnp.float32
TOP = 32767.0
LEVELS = 256.0


def halves(table):
    upper = table.astype(np.float32).astype(ml_dtypes.bfloat16)
    lower = (table - upper.astype(np.float64)).astype(np.float32)
    return upper, lower.astype(ml_dtypes.bfloat16)


def trig(rows, cols, length):
    angle = (np.outer(rows, cols) % length) * (2.0 * math.pi / length)
    return np.cos(angle), np.sin(angle)


def split(values):
    upper = values.astype(BF)
    return upper, (values - upper.astype(F32)).astype(BF)


def mul(left, right):
    return jnp.dot(left, right, preferred_element_type=F32)


def mul_t(left, right):
    return lax.dot_general(left, right, (((1,), (1,)), ((), ())), preferred_element_type=F32)


def up(value, step):
    return -(-value // step) * step


def pick_kernel(channels, block, index_ref, in_ref, out_ref):
    depth = in_ref.shape[2]
    parts = [in_ref[0, c].astype(F32) for c in range(channels)]
    if block > channels * depth:
        parts.append(jnp.zeros((block - channels * depth, in_ref.shape[3]), F32))
    out_ref[0] = jnp.concatenate(parts, axis=0).astype(BF)


def main_kernel(
    channels, planes, box, groups, rotations, length, block, rows,
    rec_hbm, own_hbm, tz_hbm, wy_ref, tx_ref, ti_ref, recv_hbm,
    rec, lbuf, tz, a_buf, b_re, b_im, spec_a, spec_b, square_a, square_b, expo, qbuf,
    load_sem, own_sem, gsend, grecv, xsend, xrecv, self_sem,
):
    me = lax.axis_index("fft")
    xs = length // groups
    sib = me + 1 - 2 * lax.rem(me, 2)
    far = [lax.rem(me + 2 * m, groups) for m in range(1, groups // 2)]
    peers = [sib] + far
    others = [lax.rem(me + s, groups) for s in range(1, groups)]
    pairs = -(-channels // 2)

    rec_copy = pltpu.make_async_copy(rec_hbm.at[:, :, pl.ds(0, planes)], rec, load_sem.at[0])
    rec_copy.start()
    tz_copy = pltpu.make_async_copy(tz_hbm.at[me], tz, load_sem.at[1])
    tz_copy.start()

    barrier = pltpu.get_barrier_semaphore()
    for peer in others:
        pl.semaphore_signal(barrier, inc=1, device_id={"fft": peer}, device_id_type=pl.DeviceIdType.MESH)
    pl.semaphore_wait(barrier, groups - 1)

    def slot(r, source):
        return lbuf.at[r, pl.ds(pl.multiple_of(source * block, block), block)]

    def own_copy(r, k):
        return pltpu.make_async_remote_copy(
            src_ref=own_hbm.at[r], dst_ref=slot(r, me), send_sem=gsend.at[r, k], recv_sem=grecv.at[r, me],
            device_id={"fft": peers[k]}, device_id_type=pl.DeviceIdType.MESH)

    def relay_copy(r, k):
        return pltpu.make_async_remote_copy(
            src_ref=slot(r, far[k]), dst_ref=slot(r, far[k]), send_sem=gsend.at[r, len(peers) + k],
            recv_sem=grecv.at[r, far[k]], device_id={"fft": sib}, device_id_type=pl.DeviceIdType.MESH)

    def arrival(r, source):
        return pltpu.make_async_remote_copy(
            src_ref=own_hbm.at[r], dst_ref=slot(r, source), send_sem=gsend.at[r, 0], recv_sem=grecv.at[r, source],
            device_id={"fft": sib}, device_id_type=pl.DeviceIdType.MESH)

    def local(r):
        return pltpu.make_async_copy(own_hbm.at[r], slot(r, me), own_sem.at[r])

    def begin(r):
        for k in range(len(peers)):
            own_copy(r, k).start()
        local(r).start()

    def relay(r):
        for k in range(len(far)):
            arrival(r, far[k]).wait_recv()
            relay_copy(r, k).start()

    def finish(r):
        arrival(r, sib).wait_recv()
        for m in range(1, groups // 2):
            arrival(r, lax.rem(sib + 2 * m, groups)).wait_recv()
        local(r).wait()

    def send_plane(r, k, s):
        peer = others[s]
        return pltpu.make_async_remote_copy(
            src_ref=qbuf.at[r, k, peer], dst_ref=recv_hbm.at[r, me, k],
            send_sem=xsend.at[r, s], recv_sem=xrecv.at[r, me],
            device_id={"fft": peer}, device_id_type=pl.DeviceIdType.MESH)

    def send_all(r, s):
        peer = others[s]
        return pltpu.make_async_remote_copy(
            src_ref=qbuf.at[r, :, peer], dst_ref=recv_hbm.at[r, peer],
            send_sem=xsend.at[r, s], recv_sem=xrecv.at[r, peer],
            device_id={"fft": peer}, device_id_type=pl.DeviceIdType.MESH)

    def keep(r):
        return pltpu.make_async_copy(
            qbuf.at[r, :, me], recv_hbm.at[r, me], self_sem.at[r])

    lanes = lax.broadcasted_iota(jnp.int32, (length, length), 1)

    def forward(r):
        finish(r)
        cells = lbuf[r]
        a_buf[...] = mul(tz[0], cells) + mul(tz[1], cells)

        @pl.when(r + 1 < rotations)
        def _():
            relay(r + 1)

        @pl.when(r + 2 < rotations)
        def _():
            begin(r + 2)

        def lane_group(j, carry):
            at = pl.ds(pl.multiple_of(j * 128, 128), 128)
            upper, lower = split(jnp.concatenate([a_buf[0:rows, at], a_buf[rows : 2 * rows, at]], axis=1))
            both = jnp.concatenate([upper, lower, upper], axis=1)
            per = 128 // box
            for i in range(per):
                out = mul(both, wy_ref[i])
                for g in range(rows // 8):
                    to = pl.ds(pl.multiple_of((g * box + j * per + i) * 8, 8), 8)
                    b_re[to, :] = out[g * 8 : g * 8 + 8, :length]
                    b_im[to, :] = out[g * 8 : g * 8 + 8, length:]
            return carry

        lax.fori_loop(0, box * box // 128, lane_group, 0)

        @pl.when(r == 0)
        def _():
            rec_copy.wait()

        def x_stage(k, spec):
            for p in range(pairs):
                pair = range(2 * p, min(2 * p + 2, channels))
                def pick(ref):
                    parts = []
                    for c in pair:
                        row = k * channels + c
                        parts.append(ref[pl.ds(row // 8 * (box * 8) + lax.rem(row, 8), box, stride=8), :])
                    return split(jnp.concatenate(parts, axis=1))
                re_hi, re_lo = pick(b_re)
                im_hi, im_lo = pick(b_im)
                right = jnp.concatenate([re_hi, im_hi, re_lo, im_lo, re_hi, im_hi], axis=0)
                spec[p, :, 0 : length * len(pair)] = mul(tx_ref[...], right)

        def product(k, spec, square):
            for h in range(0, length, 16):
                low, high = slice(h, h + 16), slice(length + h, length + h + 16)
                p_re = p_im = None
                for c in range(channels):
                    at = slice((c % 2) * length, (c % 2 + 1) * length)
                    s_re = spec[c // 2, low, at]
                    s_im = spec[c // 2, high, at]
                    r_re = rec[0, c, k, low].astype(F32)
                    r_im = rec[1, c, k, low].astype(F32)
                    q_re = r_re * s_re + r_im * s_im
                    q_im = r_im * s_re - r_re * s_im
                    p_re = q_re if p_re is None else p_re + q_re
                    p_im = q_im if p_im is None else p_im + q_im
                for t, (re, im) in enumerate(zip(split(p_re), split(p_im))):
                    square[t, low, 0:length] = re
                    square[t, low, length : 2 * length] = im
                    square[t, high, 0:length] = -im
                    square[t, high, length : 2 * length] = re

        def close(k, square):
            upper = square[0]
            field = mul(ti_ref[...], jnp.concatenate([upper, upper, square[1]], axis=0))
            most = jnp.max(jnp.abs(field), axis=1, keepdims=True)
            code = jnp.ceil(LEVELS * jnp.log2(jnp.maximum(most, 1e-30))) + 1.0
            factor = TOP * jnp.exp2(code * (-1.0 / LEVELS))
            qbuf[r, k] = jnp.round(field * factor).astype(jnp.int32).reshape(groups, xs, 2 * length).astype(jnp.int16)
            expo[...] = jnp.where(lanes == k, code, expo[...])

        def send(k):
            for s in range(groups - 1):
                send_plane(r, k, s).start()

        def two(m, carry):
            k = 2 * m
            x_stage(k - 1, spec_b)
            product(k - 2, spec_a, square_a)
            close(jnp.maximum(k - 3, 0), square_b)
            x_stage(k, spec_a)
            product(k - 1, spec_b, square_b)
            close(k - 2, square_a)

            @pl.when(m > 1)
            def _():
                send(k - 3)

            send(k - 2)
            return carry

        x_stage(0, spec_a)
        lax.fori_loop(1, planes // 2 + 1, two, 0)
        product(planes - 1, spec_a, square_a)
        close(planes - 2, square_b)
        close(planes - 1, square_a)
        send(planes - 2)
        send(planes - 1)
        codes = expo[...].astype(jnp.int32)
        codes = jnp.concatenate([codes, codes], axis=1)
        qbuf[r, planes] = codes.reshape(groups, xs, 2 * length).astype(jnp.int16)
        send(planes)
        keep(r).start()

    begin(0)
    if rotations > 1:
        begin(1)
    tz_copy.wait()
    relay(0)

    def rotation(r, carry):
        forward(r)
        return carry

    lax.fori_loop(0, rotations, rotation, 0)

    def drain(r, carry):
        for k in range(len(peers)):
            own_copy(r, k).wait_send()
        for k in range(len(far)):
            relay_copy(r, k).wait_send()
        for s in range(groups - 1):
            send_all(r, s).wait_send()
            send_all(r, s).wait_recv()
        keep(r).wait()
        return carry

    lax.fori_loop(0, rotations, drain, 0)


def final_kernel(groups, planes, length, width, terms, blocks_ref, tz_ref, tw_ref, out_ref, low_ref, f_re, f_im):
    for s in range(groups):
        code = blocks_ref[0, s, planes].astype(jnp.int32).astype(F32)[:, :length]
        scale = jnp.exp2(code * (1.0 / LEVELS)) * (1.0 / TOP)
        for k in range(planes):
            value = blocks_ref[0, s, k].astype(jnp.int32).astype(F32) * scale[:, k : k + 1]
            at = pl.ds((s * planes + k) * width, width)
            f_re[at, :] = value[:, :length]
            f_im[at, :] = value[:, length:]
    if terms > groups * planes:
        rest = pl.ds(groups * planes * width, (terms - groups * planes) * width)
        f_re[rest, :] = jnp.zeros(((terms - groups * planes) * width, length), F32)
        f_im[rest, :] = jnp.zeros(((terms - groups * planes) * width, length), F32)
    for i in range(width):
        at = pl.ds(i, terms, stride=width)
        upper, lower = split(jnp.concatenate([f_re[at, :], f_im[at, :]], axis=1))
        both = mul(tz_ref[...], jnp.concatenate([upper, lower, upper], axis=0))
        g_re = both[:length, :length] - both[length:, length:]
        g_im = both[:length, length:] + both[length:, :length]
        upper, lower = split(jnp.concatenate([g_re, g_im], axis=1))
        first = mul_t(tw_ref[...], upper)
        plane = first[:length] + first[length:] + mul_t(tw_ref[0:length], lower)
        out_ref[0, i] = plane
        low_ref[0, 0, i : i + 1, :] = jnp.min(plane, axis=0, keepdims=True)


def shards(receptor, ligand_grids, rot_index):
    groups = lax.axis_size("fft")
    channels, slab, length = receptor.shape[1], receptor.shape[2], receptor.shape[3]
    depth = ligand_grids.shape[2]
    box = depth * groups
    cells = ligand_grids.shape[3]
    rotations = rot_index.shape[0]
    xs = length // groups
    planes = slab // 2 + 1
    block = up(channels * depth, 16)
    rows = up(planes * channels, 16)
    freq = np.arange(length)

    t_z = np.zeros((groups, 2, rows, groups, block))
    for d in range(groups):
        cz, sz = trig(d * slab + np.arange(planes), np.arange(box), length)
        for c in range(channels):
            at = np.arange(planes) * channels + c
            for s in range(groups):
                span = slice(c * depth, (c + 1) * depth)
                cut = slice(s * depth, (s + 1) * depth)
                t_z[d, 0, at, s, span] = cz[:, cut]
                t_z[d, 1, at, s, span] = -sz[:, cut]
    t_z = t_z.reshape(groups, 2 * rows, groups * block)
    t_z = jnp.asarray(np.stack(halves(t_z), axis=1))

    cy, sy = trig(np.arange(box), freq, length)
    per = 128 // box
    w_y = np.zeros((per, 256, 2 * length))
    for i in range(per):
        w_y[i, i * box : (i + 1) * box] = np.concatenate([cy, -sy], axis=1)
        w_y[i, 128 + i * box : 128 + (i + 1) * box] = np.concatenate([sy, cy], axis=1)
    hi, lo = halves(w_y)
    w_y = jnp.asarray(np.concatenate([hi, hi, lo], axis=1))

    t_x = np.block([[cy.T, sy.T], [-sy.T, cy.T]])
    hi, lo = halves(t_x)
    t_x = jnp.asarray(np.concatenate([hi, hi, lo], axis=1))

    cf, sf = trig(freq, freq, length)
    hi, lo = halves(np.concatenate([cf, sf], axis=1))
    t_i = jnp.asarray(np.concatenate([hi, lo, hi], axis=1))

    terms = up(groups * planes, 16)
    kz = np.zeros(terms, np.int64)
    weight = np.zeros(terms)
    for d in range(groups):
        for k in range(planes):
            f = d * slab + k
            kz[d * planes + k] = f
            if d < groups // 2:
                used = k < slab // 2
            else:
                used = k > 0 or f == length // 2
            weight[d * planes + k] = 0.0 if not used else 1.0 if f in (0, length // 2) else 2.0
    cb, sb = trig(freq, kz, length)
    hi, lo = halves(np.concatenate([cb * weight, sb * weight], axis=0))
    t_b = jnp.asarray(np.concatenate([hi, hi, lo], axis=1))
    t_w = jnp.asarray(np.concatenate(halves(np.concatenate([cf, -sf], axis=1) / float(length) ** 3), axis=0))

    own = pl.pallas_call(
        functools.partial(pick_kernel, channels, block),
        grid_spec=pltpu.PrefetchScalarGridSpec(
            num_scalar_prefetch=1,
            grid=(rotations,),
            in_specs=[pl.BlockSpec((1, channels, depth, cells), lambda r, index: (index[r], 0, 0, 0))],
            out_specs=pl.BlockSpec((1, block, cells), lambda r, index: (r, 0, 0)),
        ),
        out_shape=jax.ShapeDtypeStruct((rotations, block, cells), BF),
    )(rot_index, ligand_grids)

    any_space = pl.BlockSpec(memory_space=pl.ANY)
    vmem = pl.BlockSpec(memory_space=pltpu.VMEM)
    sent = pl.pallas_call(
        functools.partial(main_kernel, channels, planes, box, groups, rotations, length, block, rows),
        in_specs=[any_space, any_space, any_space, vmem, vmem, vmem],
        out_specs=any_space,
        out_shape=jax.ShapeDtypeStruct((rotations, groups, planes + 1, xs, 2 * length), jnp.int16),
        scratch_shapes=[
            pltpu.VMEM((2, channels, planes, length, length), BF),
            pltpu.VMEM((rotations, groups * block, cells), BF),
            pltpu.VMEM((2, 2 * rows, groups * block), BF),
            pltpu.VMEM((2 * rows, cells), F32),
            pltpu.VMEM((rows * box, length), F32),
            pltpu.VMEM((rows * box, length), F32),
            pltpu.VMEM((-(-channels // 2), 2 * length, 2 * length), F32),
            pltpu.VMEM((-(-channels // 2), 2 * length, 2 * length), F32),
            pltpu.VMEM((2, 2 * length, 2 * length), BF),
            pltpu.VMEM((2, 2 * length, 2 * length), BF),
            pltpu.VMEM((length, length), F32),
            pltpu.VMEM((rotations, planes + 1, groups, xs, 2 * length), jnp.int16),
            pltpu.SemaphoreType.DMA((2,)),
            pltpu.SemaphoreType.DMA((rotations,)),
            pltpu.SemaphoreType.DMA((rotations, groups)),
            pltpu.SemaphoreType.DMA((rotations, groups)),
            pltpu.SemaphoreType.DMA((rotations, groups)),
            pltpu.SemaphoreType.DMA((rotations, groups)),
            pltpu.SemaphoreType.DMA((rotations,)),
        ],
        compiler_params=pltpu.CompilerParams(
            collective_id=0, has_side_effects=True, vmem_limit_bytes=56 * 2**20),
        cost_estimate=pl.CostEstimate(flops=rotations * 6 * 10**9, bytes_accessed=30_000_000, transcendentals=0),
    )(receptor, own, t_z, w_y, t_x, t_i)

    width = min(16, xs)
    scores, lows = pl.pallas_call(
        functools.partial(final_kernel, groups, planes, length, width, terms),
        grid=(rotations, xs // width),
        in_specs=[
            pl.BlockSpec((1, groups, planes + 1, width, 2 * length), lambda r, x: (r, 0, 0, x, 0)),
            pl.BlockSpec(t_b.shape, lambda r, x: (0, 0)),
            pl.BlockSpec(t_w.shape, lambda r, x: (0, 0)),
        ],
        out_specs=[
            pl.BlockSpec((1, width, length, length), lambda r, x: (r, x, 0, 0)),
            pl.BlockSpec((1, 1, width, length), lambda r, x: (r, x, 0, 0)),
        ],
        out_shape=[
            jax.ShapeDtypeStruct((rotations, xs, length, length), F32),
            jax.ShapeDtypeStruct((rotations, xs // width, width, length), F32),
        ],
        scratch_shapes=[pltpu.VMEM((terms * width, length), F32)] * 2,
        compiler_params=pltpu.CompilerParams(vmem_limit_bytes=32 * 2**20),
        cost_estimate=pl.CostEstimate(flops=rotations * 10**9, bytes_accessed=20_000_000, transcendentals=0),
    )(sent, t_b, t_w)
    best = lax.pmin(jnp.min(lows, axis=(1, 2, 3)), "fft")
    return scores, best


def solution(mesh):
    placed = (P(None, None, "fft", None, None), P(None, None, "fft", None), P("rot"))
    return jax.shard_map(
        shards,
        mesh=mesh,
        in_specs=placed,
        out_specs=(P("rot", "fft", None, None), P("rot")),
        check_vma=False,
    )
```

```python
import functools
import math

import jax
import jax.numpy as jnp
import ml_dtypes
import numpy as np
from jax import lax
from jax.experimental import pallas as pl
from jax.experimental.pallas import tpu as pltpu
from jax.sharding import PartitionSpec as P

BF = jnp.bfloat16
F32 = jnp.float32
TOP = 32767.0
LEVELS = 256.0


def halves(table):
    upper = table.astype(np.float32).astype(ml_dtypes.bfloat16)
    lower = (table - upper.astype(np.float64)).astype(np.float32)
    return upper, lower.astype(ml_dtypes.bfloat16)


def trig(rows, cols, length):
    angle = (np.outer(rows, cols) % length) * (2.0 * math.pi / length)
    return np.cos(angle), np.sin(angle)


def split(values):
    upper = values.astype(BF)
    return upper, (values - upper.astype(F32)).astype(BF)


def mul(left, right):
    return jnp.dot(left, right, preferred_element_type=F32)


def mul_t(left, right):
    return lax.dot_general(left, right, (((1,), (1,)), ((), ())), preferred_element_type=F32)


def up(value, step):
    return -(-value // step) * step


def pick_kernel(channels, block, index_ref, in_ref, out_ref):
    depth = in_ref.shape[2]
    parts = [in_ref[0, c].astype(F32) for c in range(channels)]
    if block > channels * depth:
        parts.append(jnp.zeros((block - channels * depth, in_ref.shape[3]), F32))
    out_ref[0] = jnp.concatenate(parts, axis=0).astype(BF)


def main_kernel(
    channels, planes, box, groups, rotations, length, block, rows,
    rec_hbm, own_hbm, tz_hbm, wy_ref, tx_ref, ti_ref, recv_hbm,
    rec, lbuf, tz, a_buf, b_re, b_im, spec_a, spec_b, square_a, square_b, expo, qbuf,
    load_sem, own_sem, gsend, grecv, xsend, xrecv, self_sem,
):
    me = lax.axis_index("fft")
    xs = length // groups
    sib = me + 1 - 2 * lax.rem(me, 2)
    far = [lax.rem(me + 2 * m, groups) for m in range(1, groups // 2)]
    peers = [sib] + far
    others = [lax.rem(me + s, groups) for s in range(1, groups)]
    pairs = -(-channels // 2)

    rec_copy = pltpu.make_async_copy(rec_hbm.at[:, :, pl.ds(0, planes)], rec, load_sem.at[0])
    rec_copy.start()
    tz_copy = pltpu.make_async_copy(tz_hbm.at[me], tz, load_sem.at[1])
    tz_copy.start()

    barrier = pltpu.get_barrier_semaphore()
    for peer in others:
        pl.semaphore_signal(barrier, inc=1, device_id={"fft": peer}, device_id_type=pl.DeviceIdType.MESH)
    pl.semaphore_wait(barrier, groups - 1)

    def slot(r, source):
        return lbuf.at[r, pl.ds(pl.multiple_of(source * block, block), block)]

    def own_copy(r, k):
        return pltpu.make_async_remote_copy(
            src_ref=own_hbm.at[r], dst_ref=slot(r, me), send_sem=gsend.at[r, k], recv_sem=grecv.at[r, me],
            device_id={"fft": peers[k]}, device_id_type=pl.DeviceIdType.MESH)

    def relay_copy(r, k):
        return pltpu.make_async_remote_copy(
            src_ref=slot(r, far[k]), dst_ref=slot(r, far[k]), send_sem=gsend.at[r, len(peers) + k],
            recv_sem=grecv.at[r, far[k]], device_id={"fft": sib}, device_id_type=pl.DeviceIdType.MESH)

    def arrival(r, source):
        return pltpu.make_async_remote_copy(
            src_ref=own_hbm.at[r], dst_ref=slot(r, source), send_sem=gsend.at[r, 0], recv_sem=grecv.at[r, source],
            device_id={"fft": sib}, device_id_type=pl.DeviceIdType.MESH)

    def local(r):
        return pltpu.make_async_copy(own_hbm.at[r], slot(r, me), own_sem.at[r])

    def begin(r):
        for k in range(len(peers)):
            own_copy(r, k).start()
        local(r).start()

    def relay(r):
        for k in range(len(far)):
            arrival(r, far[k]).wait_recv()
            relay_copy(r, k).start()

    def finish(r):
        arrival(r, sib).wait_recv()
        for m in range(1, groups // 2):
            arrival(r, lax.rem(sib + 2 * m, groups)).wait_recv()
        local(r).wait()

    def send_plane(r, k, s):
        peer = others[s]
        return pltpu.make_async_remote_copy(
            src_ref=qbuf.at[r, k, peer], dst_ref=recv_hbm.at[r, me, k],
            send_sem=xsend.at[r, s], recv_sem=xrecv.at[r, me],
            device_id={"fft": peer}, device_id_type=pl.DeviceIdType.MESH)

    def send_all(r, s):
        peer = others[s]
        return pltpu.make_async_remote_copy(
            src_ref=qbuf.at[r, :, peer], dst_ref=recv_hbm.at[r, peer],
            send_sem=xsend.at[r, s], recv_sem=xrecv.at[r, peer],
            device_id={"fft": peer}, device_id_type=pl.DeviceIdType.MESH)

    def keep(r):
        return pltpu.make_async_copy(
            qbuf.at[r, :, me], recv_hbm.at[r, me], self_sem.at[r])

    lanes = lax.broadcasted_iota(jnp.int32, (length, length), 1)

    def forward(r):
        finish(r)
        cells = lbuf[r]
        a_buf[...] = mul(tz[0], cells) + mul(tz[1], cells)

        @pl.when(r + 1 < rotations)
        def _():
            relay(r + 1)

        @pl.when(r + 2 < rotations)
        def _():
            begin(r + 2)

        def lane_group(j, carry):
            at = pl.ds(pl.multiple_of(j * 128, 128), 128)
            upper, lower = split(jnp.concatenate([a_buf[0:rows, at], a_buf[rows : 2 * rows, at]], axis=1))
            both = jnp.concatenate([upper, lower, upper], axis=1)
            per = 128 // box
            for i in range(per):
                out = mul(both, wy_ref[i])
                for g in range(rows // 8):
                    to = pl.ds(pl.multiple_of((g * box + j * per + i) * 8, 8), 8)
                    b_re[to, :] = out[g * 8 : g * 8 + 8, :length]
                    b_im[to, :] = out[g * 8 : g * 8 + 8, length:]
            return carry

        lax.fori_loop(0, box * box // 128, lane_group, 0)

        @pl.when(r == 0)
        def _():
            rec_copy.wait()

        def x_stage(k, spec):
            for p in range(pairs):
                pair = range(2 * p, min(2 * p + 2, channels))
                def pick(ref):
                    parts = []
                    for c in pair:
                        row = k * channels + c
                        parts.append(ref[pl.ds(row // 8 * (box * 8) + lax.rem(row, 8), box, stride=8), :])
                    return split(jnp.concatenate(parts, axis=1))
                re_hi, re_lo = pick(b_re)
                im_hi, im_lo = pick(b_im)
                right = jnp.concatenate([re_hi, im_hi, re_lo, im_lo, re_hi, im_hi], axis=0)
                spec[p, :, 0 : length * len(pair)] = mul(tx_ref[...], right)

        def product(k, spec, square):
            for h in range(0, length, 16):
                low, high = slice(h, h + 16), slice(length + h, length + h + 16)
                p_re = p_im = None
                for c in range(channels):
                    at = slice((c % 2) * length, (c % 2 + 1) * length)
                    s_re = spec[c // 2, low, at]
                    s_im = spec[c // 2, high, at]
                    r_re = rec[0, c, k, low].astype(F32)
                    r_im = rec[1, c, k, low].astype(F32)
                    q_re = r_re * s_re + r_im * s_im
                    q_im = r_im * s_re - r_re * s_im
                    p_re = q_re if p_re is None else p_re + q_re
                    p_im = q_im if p_im is None else p_im + q_im
                for t, (re, im) in enumerate(zip(split(p_re), split(p_im))):
                    square[t, low, 0:length] = re
                    square[t, low, length : 2 * length] = im
                    square[t, high, 0:length] = -im
                    square[t, high, length : 2 * length] = re

        def close(k, square):
            upper = square[0]
            field = mul(ti_ref[...], jnp.concatenate([upper, upper, square[1]], axis=0))
            most = jnp.max(jnp.abs(field), axis=1, keepdims=True)
            code = jnp.ceil(LEVELS * jnp.log2(jnp.maximum(most, 1e-30))) + 1.0
            factor = TOP * jnp.exp2(code * (-1.0 / LEVELS))
            qbuf[r, k] = jnp.round(field * factor).astype(jnp.int32).reshape(groups, xs, 2 * length).astype(jnp.int16)
            expo[...] = jnp.where(lanes == k, code, expo[...])

        def send(k):
            for s in range(groups - 1):
                send_plane(r, k, s).start()

        def two(m, carry):
            k = 2 * m
            x_stage(k - 1, spec_b)
            product(k - 2, spec_a, square_a)
            close(jnp.maximum(k - 3, 0), square_b)
            x_stage(k, spec_a)
            product(k - 1, spec_b, square_b)
            close(k - 2, square_a)

            @pl.when(m > 1)
            def _():
                send(k - 3)

            send(k - 2)
            return carry

        x_stage(0, spec_a)
        lax.fori_loop(1, planes // 2 + 1, two, 0)
        product(planes - 1, spec_a, square_a)
        close(planes - 2, square_b)
        close(planes - 1, square_a)
        send(planes - 2)
        send(planes - 1)
        codes = expo[...].astype(jnp.int32)
        codes = jnp.concatenate([codes, codes], axis=1)
        qbuf[r, planes] = codes.reshape(groups, xs, 2 * length).astype(jnp.int16)
        send(planes)
        keep(r).start()

    begin(0)
    if rotations > 1:
        begin(1)
    tz_copy.wait()
    relay(0)

    def rotation(r, carry):
        forward(r)
        return carry

    lax.fori_loop(0, rotations, rotation, 0)

    def drain(r, carry):
        for k in range(len(peers)):
            own_copy(r, k).wait_send()
        for k in range(len(far)):
            relay_copy(r, k).wait_send()
        for s in range(groups - 1):
            send_all(r, s).wait_send()
            send_all(r, s).wait_recv()
        keep(r).wait()
        return carry

    lax.fori_loop(0, rotations, drain, 0)


def final_kernel(groups, planes, length, width, terms, blocks_ref, ty_ref, tz_ref, out_ref, low_ref, h_re, h_im):
    for s in range(groups):
        code = blocks_ref[0, s, planes].astype(jnp.int32).astype(F32)[:, :length]
        scale = jnp.exp2(code * (1.0 / LEVELS)) * (1.0 / TOP)
        parts = [blocks_ref[0, s, k].astype(jnp.int32).astype(F32) * scale[:, k : k + 1] for k in range(planes)]
        upper, lower = split(jnp.concatenate(parts, axis=0))
        lines = mul(jnp.concatenate([upper, upper, lower], axis=1), ty_ref[...])
        at = pl.ds(s * planes * width, planes * width)
        h_re[at, :] = lines[:, :length]
        h_im[at, :] = lines[:, length:]
    if terms > groups * planes:
        rest = pl.ds(groups * planes * width, (terms - groups * planes) * width)
        h_re[rest, :] = jnp.zeros(((terms - groups * planes) * width, length), F32)
        h_im[rest, :] = jnp.zeros(((terms - groups * planes) * width, length), F32)
    for i in range(0, width, 2):
        def both(ref):
            return split(jnp.concatenate([ref[pl.ds(i + t, terms, stride=width), :] for t in range(2)], axis=1))
        re_hi, re_lo = both(h_re)
        im_hi, im_lo = both(h_im)
        right = jnp.concatenate([re_hi, im_hi, re_lo, im_lo, re_hi, im_hi], axis=0)
        field = mul(tz_ref[...], right)
        for t in range(2):
            plane = field[:, t * length : (t + 1) * length]
            low_ref[0, 0, i + t : i + t + 1, :] = jnp.min(plane, axis=0, keepdims=True)
            out_ref[0, i + t] = plane.T


def shards(receptor, ligand_grids, rot_index):
    groups = lax.axis_size("fft")
    channels, slab, length = receptor.shape[1], receptor.shape[2], receptor.shape[3]
    depth = ligand_grids.shape[2]
    box = depth * groups
    cells = ligand_grids.shape[3]
    rotations = rot_index.shape[0]
    xs = length // groups
    planes = slab // 2 + 1
    block = up(channels * depth, 16)
    rows = up(planes * channels, 16)
    freq = np.arange(length)

    t_z = np.zeros((groups, 2, rows, groups, block))
    for d in range(groups):
        cz, sz = trig(d * slab + np.arange(planes), np.arange(box), length)
        for c in range(channels):
            at = np.arange(planes) * channels + c
            for s in range(groups):
                span = slice(c * depth, (c + 1) * depth)
                cut = slice(s * depth, (s + 1) * depth)
                t_z[d, 0, at, s, span] = cz[:, cut]
                t_z[d, 1, at, s, span] = -sz[:, cut]
    t_z = t_z.reshape(groups, 2 * rows, groups * block)
    t_z = jnp.asarray(np.stack(halves(t_z), axis=1))

    cy, sy = trig(np.arange(box), freq, length)
    per = 128 // box
    w_y = np.zeros((per, 256, 2 * length))
    for i in range(per):
        w_y[i, i * box : (i + 1) * box] = np.concatenate([cy, -sy], axis=1)
        w_y[i, 128 + i * box : 128 + (i + 1) * box] = np.concatenate([sy, cy], axis=1)
    hi, lo = halves(w_y)
    w_y = jnp.asarray(np.concatenate([hi, hi, lo], axis=1))

    t_x = np.block([[cy.T, sy.T], [-sy.T, cy.T]])
    hi, lo = halves(t_x)
    t_x = jnp.asarray(np.concatenate([hi, hi, lo], axis=1))

    cf, sf = trig(freq, freq, length)
    hi, lo = halves(np.concatenate([cf, sf], axis=1))
    t_i = jnp.asarray(np.concatenate([hi, lo, hi], axis=1))

    terms = up(groups * planes, 16)
    kz = np.zeros(terms, np.int64)
    weight = np.zeros(terms)
    for d in range(groups):
        for k in range(planes):
            f = d * slab + k
            kz[d * planes + k] = f
            if d < groups // 2:
                used = k < slab // 2
            else:
                used = k > 0 or f == length // 2
            weight[d * planes + k] = 0.0 if not used else 1.0 if f in (0, length // 2) else 2.0
    cb, sb = trig(freq, kz, length)
    hi, lo = halves(np.concatenate([cb * weight, -sb * weight], axis=1))
    t_b = jnp.asarray(np.concatenate([hi, hi, lo], axis=1))
    hi, lo = halves(np.block([[cf, sf], [-sf, cf]]) / float(length) ** 3)
    t_w = jnp.asarray(np.concatenate([hi, lo, hi], axis=0))

    own = pl.pallas_call(
        functools.partial(pick_kernel, channels, block),
        grid_spec=pltpu.PrefetchScalarGridSpec(
            num_scalar_prefetch=1,
            grid=(rotations,),
            in_specs=[pl.BlockSpec((1, channels, depth, cells), lambda r, index: (index[r], 0, 0, 0))],
            out_specs=pl.BlockSpec((1, block, cells), lambda r, index: (r, 0, 0)),
        ),
        out_shape=jax.ShapeDtypeStruct((rotations, block, cells), BF),
    )(rot_index, ligand_grids)

    any_space = pl.BlockSpec(memory_space=pl.ANY)
    vmem = pl.BlockSpec(memory_space=pltpu.VMEM)
    sent = pl.pallas_call(
        functools.partial(main_kernel, channels, planes, box, groups, rotations, length, block, rows),
        in_specs=[any_space, any_space, any_space, vmem, vmem, vmem],
        out_specs=any_space,
        out_shape=jax.ShapeDtypeStruct((rotations, groups, planes + 1, xs, 2 * length), jnp.int16),
        scratch_shapes=[
            pltpu.VMEM((2, channels, planes, length, length), BF),
            pltpu.VMEM((rotations, groups * block, cells), BF),
            pltpu.VMEM((2, 2 * rows, groups * block), BF),
            pltpu.VMEM((2 * rows, cells), F32),
            pltpu.VMEM((rows * box, length), F32),
            pltpu.VMEM((rows * box, length), F32),
            pltpu.VMEM((-(-channels // 2), 2 * length, 2 * length), F32),
            pltpu.VMEM((-(-channels // 2), 2 * length, 2 * length), F32),
            pltpu.VMEM((2, 2 * length, 2 * length), BF),
            pltpu.VMEM((2, 2 * length, 2 * length), BF),
            pltpu.VMEM((length, length), F32),
            pltpu.VMEM((rotations, planes + 1, groups, xs, 2 * length), jnp.int16),
            pltpu.SemaphoreType.DMA((2,)),
            pltpu.SemaphoreType.DMA((rotations,)),
            pltpu.SemaphoreType.DMA((rotations, groups)),
            pltpu.SemaphoreType.DMA((rotations, groups)),
            pltpu.SemaphoreType.DMA((rotations, groups)),
            pltpu.SemaphoreType.DMA((rotations, groups)),
            pltpu.SemaphoreType.DMA((rotations,)),
        ],
        compiler_params=pltpu.CompilerParams(
            collective_id=0, has_side_effects=True, vmem_limit_bytes=56 * 2**20),
        cost_estimate=pl.CostEstimate(flops=rotations * 6 * 10**9, bytes_accessed=30_000_000, transcendentals=0),
    )(receptor, own, t_z, w_y, t_x, t_i)

    width = min(16, xs)
    scores, lows = pl.pallas_call(
        functools.partial(final_kernel, groups, planes, length, width, terms),
        grid=(rotations, xs // width),
        in_specs=[
            pl.BlockSpec((1, groups, planes + 1, width, 2 * length), lambda r, x: (r, 0, 0, x, 0)),
            pl.BlockSpec(t_w.shape, lambda r, x: (0, 0)),
            pl.BlockSpec(t_b.shape, lambda r, x: (0, 0)),
        ],
        out_specs=[
            pl.BlockSpec((1, width, length, length), lambda r, x: (r, x, 0, 0)),
            pl.BlockSpec((1, 1, width, length), lambda r, x: (r, x, 0, 0)),
        ],
        out_shape=[
            jax.ShapeDtypeStruct((rotations, xs, length, length), F32),
            jax.ShapeDtypeStruct((rotations, xs // width, width, length), F32),
        ],
        scratch_shapes=[pltpu.VMEM((terms * width, length), F32)] * 2,
        compiler_params=pltpu.CompilerParams(vmem_limit_bytes=32 * 2**20),
        cost_estimate=pl.CostEstimate(flops=rotations * 10**9, bytes_accessed=20_000_000, transcendentals=0),
    )(sent, t_w, t_b)
    best = lax.pmin(jnp.min(lows, axis=(1, 2, 3)), "fft")
    return scores, best


def solution(mesh):
    placed = (P(None, None, "fft", None, None), P(None, None, "fft", None), P("rot"))
    return jax.shard_map(
        shards,
        mesh=mesh,
        in_specs=placed,
        out_specs=(P("rot", "fft", None, None), P("rot")),
        check_vma=False,
    )
```

```python
import functools
import math

import jax
import jax.numpy as jnp
import ml_dtypes
import numpy as np
from jax import lax
from jax.experimental import pallas as pl
from jax.experimental.pallas import tpu as pltpu
from jax.sharding import PartitionSpec as P

BF = jnp.bfloat16
F32 = jnp.float32
TOP = 32767.0
LEVELS = 256.0


def halves(table):
    upper = table.astype(np.float32).astype(ml_dtypes.bfloat16)
    lower = (table - upper.astype(np.float64)).astype(np.float32)
    return upper, lower.astype(ml_dtypes.bfloat16)


def trig(rows, cols, length):
    angle = (np.outer(rows, cols) % length) * (2.0 * math.pi / length)
    return np.cos(angle), np.sin(angle)


def split(values):
    upper = values.astype(BF)
    return upper, (values - upper.astype(F32)).astype(BF)


def mul(left, right):
    return jnp.dot(left, right, preferred_element_type=F32)


def mul_t(left, right):
    return lax.dot_general(left, right, (((1,), (1,)), ((), ())), preferred_element_type=F32)


def up(value, step):
    return -(-value // step) * step


def pick_kernel(cuts, index_ref, in_ref, out_ref):
    depth, cells = in_ref.shape[2], in_ref.shape[3]
    parts = []
    for start, stop, size in cuts:
        parts += [in_ref[0, c].astype(F32) for c in range(start, stop)]
        if size > (stop - start) * depth:
            parts.append(jnp.zeros((size - (stop - start) * depth, cells), F32))
    out_ref[0] = jnp.concatenate(parts, axis=0).astype(BF)


def main_kernel(
    channels, planes, box, groups, rotations, length, cuts, tops,
    rec_hbm, own_hbm, tza_hbm, tzb_hbm, wy_ref, tx_ref, ti_ref, recv_hbm,
    rec, stage, lbuf, tza, tzb, a_buf, even_re, even_im, odd_re, odd_im, spec_a, spec_b, square_a, square_b, expo, qbuf,
    load_sem, own_sem, gsend, grecv, xsend, xrecv, self_sem,
):
    me = lax.axis_index("fft")
    block = cuts[0][2] + cuts[1][2]
    rows = tops[0] + tops[1]
    middle = cuts[1][0]
    xs = length // groups
    sib = me + 1 - 2 * lax.rem(me, 2)
    far = [lax.rem(me + 2 * m, groups) for m in range(1, groups // 2)]
    peers = [sib] + far
    others = [lax.rem(me + s, groups) for s in range(1, groups)]
    pairs = -(-channels // 2)

    def fetch(k):
        slot_at = lax.rem(k, 2)
        return pltpu.make_async_copy(rec_hbm.at[:, :, k], stage.at[slot_at], load_sem.at[slot_at])

    fetch(0).start()
    table_copies = [
        pltpu.make_async_copy(tza_hbm.at[me], tza, load_sem.at[2]),
        pltpu.make_async_copy(tzb_hbm.at[me], tzb, load_sem.at[3]),
    ]
    for copy in table_copies:
        copy.start()

    barrier = pltpu.get_barrier_semaphore()
    for peer in others:
        pl.semaphore_signal(barrier, inc=1, device_id={"fft": peer}, device_id_type=pl.DeviceIdType.MESH)
    pl.semaphore_wait(barrier, groups - 1)

    def slot(r, source):
        return lbuf.at[r, pl.ds(pl.multiple_of(source * block, block), block)]

    def own_copy(r, k):
        return pltpu.make_async_remote_copy(
            src_ref=own_hbm.at[r], dst_ref=slot(r, me), send_sem=gsend.at[r, k], recv_sem=grecv.at[r, me],
            device_id={"fft": peers[k]}, device_id_type=pl.DeviceIdType.MESH)

    def relay_copy(r, k):
        return pltpu.make_async_remote_copy(
            src_ref=slot(r, far[k]), dst_ref=slot(r, far[k]), send_sem=gsend.at[r, len(peers) + k],
            recv_sem=grecv.at[r, far[k]], device_id={"fft": sib}, device_id_type=pl.DeviceIdType.MESH)

    def arrival(r, source):
        return pltpu.make_async_remote_copy(
            src_ref=own_hbm.at[r], dst_ref=slot(r, source), send_sem=gsend.at[r, 0], recv_sem=grecv.at[r, source],
            device_id={"fft": sib}, device_id_type=pl.DeviceIdType.MESH)

    def local(r):
        return pltpu.make_async_copy(own_hbm.at[r], slot(r, me), own_sem.at[r])

    def begin(r):
        for k in range(len(peers)):
            own_copy(r, k).start()
        local(r).start()

    def relay(r):
        for k in range(len(far)):
            arrival(r, far[k]).wait_recv()
            relay_copy(r, k).start()

    def finish(r):
        arrival(r, sib).wait_recv()
        for m in range(1, groups // 2):
            arrival(r, lax.rem(sib + 2 * m, groups)).wait_recv()
        local(r).wait()

    def send_plane(r, k, s):
        peer = others[s]
        return pltpu.make_async_remote_copy(
            src_ref=qbuf.at[lax.rem(r, 2), k, peer], dst_ref=recv_hbm.at[r, me, k],
            send_sem=xsend.at[r, s], recv_sem=xrecv.at[r, me],
            device_id={"fft": peer}, device_id_type=pl.DeviceIdType.MESH)

    def send_all(r, s):
        peer = others[s]
        return pltpu.make_async_remote_copy(
            src_ref=qbuf.at[lax.rem(r, 2), :, peer], dst_ref=recv_hbm.at[r, peer],
            send_sem=xsend.at[r, s], recv_sem=xrecv.at[r, peer],
            device_id={"fft": peer}, device_id_type=pl.DeviceIdType.MESH)

    def keep(r):
        return pltpu.make_async_copy(
            qbuf.at[lax.rem(r, 2), :, me], recv_hbm.at[r, me], self_sem.at[r])

    lanes = lax.broadcasted_iota(jnp.int32, (length, length), 1)

    per = 128 // box
    lane_groups = box * box // 128

    def z_stage(r):
        for half, table in enumerate((tza, tzb)):
            skip, size, top = half * cuts[0][2], cuts[half][2], tops[half]
            cells = jnp.concatenate([lbuf[r, s * block + skip : s * block + skip + size] for s in range(groups)], axis=0)
            out = mul(table[0], cells) + mul(table[1], cells)
            to = half * tops[0]
            a_buf[to : to + top] = out[:top]
            a_buf[rows + to : rows + to + top] = out[top:]

    first_lanes = lax.broadcasted_iota(jnp.int32, (rows, 128), 1) < 64

    def lane_group(j, b_re, b_im):
        at = pl.ds(pl.multiple_of(j * 128, 128), 128)
        whole, early, late = [], [], []
        for values in (a_buf[0:rows, at], a_buf[rows : 2 * rows, at]):
            upper = values.astype(BF)
            wide = upper.astype(F32)
            lower = pltpu.roll(values - wide, 64, 1)
            whole.append(upper)
            early.append(jnp.where(first_lanes, wide, lower).astype(BF))
            late.append(jnp.where(first_lanes, lower, wide).astype(BF))
        for i in range(per):
            out = mul(jnp.concatenate((early if i < per // 2 else late) + whole, axis=1), wy_ref[i])
            for g in range(rows // 8):
                to = pl.ds(pl.multiple_of((g * box + j * per + i) * 8, 8), 8)
                b_re[to, :] = out[g * 8 : g * 8 + 8, :length]
                b_im[to, :] = out[g * 8 : g * 8 + 8, length:]

    def release(r):
        for s in range(groups - 1):
            send_all(r, s).wait_send()
        keep(r).wait()

    def forward(r, b_re, b_im, next_re, next_im):
        q = lax.rem(r, 2)

        @pl.when(r + 1 < rotations)
        def _():
            finish(r + 1)

        z_stage(jnp.minimum(r + 1, rotations - 1))

        @pl.when(r + 2 < rotations)
        def _():
            relay(r + 2)

        @pl.when(r + 3 < rotations)
        def _():
            begin(r + 3)

        @pl.when(r >= 2)
        def _():
            release(r - 2)

        def x_stage(k, spec):
            for p in range(pairs):
                pair = range(2 * p, min(2 * p + 2, channels))
                def pick(ref):
                    parts = []
                    for c in pair:
                        row = k * middle + c if c < middle else tops[0] + k * (channels - middle) + c - middle
                        parts.append(ref[pl.ds(row // 8 * (box * 8) + lax.rem(row, 8), box, stride=8), :])
                    return split(jnp.concatenate(parts, axis=1))
                re_hi, re_lo = pick(b_re)
                im_hi, im_lo = pick(b_im)
                right = jnp.concatenate([re_hi, im_hi, re_lo, im_lo, re_hi, im_hi], axis=0)
                spec[p, :, 0 : length * len(pair)] = mul(tx_ref[...], right)

        def product(k, spec, square):
            for h in range(0, length, 16):
                low, high = slice(h, h + 16), slice(length + h, length + h + 16)
                p_re = p_im = None
                for c in range(channels):
                    at = slice((c % 2) * length, (c % 2 + 1) * length)
                    s_re = spec[c // 2, low, at]
                    s_im = spec[c // 2, high, at]
                    r_re = rec[0, c, k, low]
                    r_im = rec[1, c, k, low]
                    q_re = r_re * s_re + r_im * s_im
                    q_im = r_im * s_re - r_re * s_im
                    p_re = q_re if p_re is None else p_re + q_re
                    p_im = q_im if p_im is None else p_im + q_im
                for t, (re, im) in enumerate(zip(split(p_re), split(p_im))):
                    square[t, low, 0:length] = re
                    square[t, low, length : 2 * length] = im
                    square[t, high, 0:length] = -im
                    square[t, high, length : 2 * length] = re

        def close(k, square):
            upper = square[0]
            field = mul(ti_ref[...], jnp.concatenate([upper, upper, square[1]], axis=0))
            most = jnp.max(jnp.abs(field), axis=1, keepdims=True)
            code = jnp.ceil(LEVELS * jnp.log2(jnp.maximum(most, 1e-30))) + 1.0
            factor = TOP * jnp.exp2(code * (-1.0 / LEVELS))
            qbuf[q, k] = jnp.round(field * factor).astype(jnp.int32).reshape(groups, xs, 2 * length).astype(jnp.int16)
            expo[...] = jnp.where(lanes == k, code, expo[...])

        def send(k):
            for s in range(groups - 1):
                send_plane(r, k, s).start()

        each = -(-lane_groups // (planes // 2))

        def two(m, carry):
            k = 2 * m
            x_stage(k - 1, spec_b)
            for g in range(each):
                lane_group(jnp.minimum((m - 1) * each + g, lane_groups - 1), next_re, next_im)
            product(k - 2, spec_a, square_a)
            close(jnp.maximum(k - 3, 0), square_b)
            x_stage(k, spec_a)
            product(k - 1, spec_b, square_b)
            close(k - 2, square_a)

            @pl.when(m > 1)
            def _():
                send(k - 3)

            send(k - 2)
            return carry

        x_stage(0, spec_a)
        lax.fori_loop(1, planes // 2 + 1, two, 0)
        product(planes - 1, spec_a, square_a)
        close(planes - 2, square_b)
        close(planes - 1, square_a)
        send(planes - 2)
        send(planes - 1)
        codes = expo[...].astype(jnp.int32)
        codes = jnp.concatenate([codes, codes], axis=1)
        qbuf[q, planes] = codes.reshape(groups, xs, 2 * length).astype(jnp.int16)
        send(planes)
        keep(r).start()

    for r in range(min(3, rotations)):
        begin(r)

    def widen(k, carry):
        @pl.when(k + 1 < planes)
        def _():
            fetch(k + 1).start()

        fetch(k).wait()
        for part in range(2):
            for c in range(channels):
                rec[part, c, k] = stage[lax.rem(k, 2), part, c].astype(F32)
        return carry

    lax.fori_loop(0, planes, widen, 0)
    for copy in table_copies:
        copy.wait()
    relay(0)
    finish(0)
    z_stage(0)
    if rotations > 1:
        relay(1)

    def first(j, carry):
        lane_group(j, even_re, even_im)
        return carry

    lax.fori_loop(0, lane_groups, first, 0)

    def rotation_pair(p, carry):
        forward(2 * p, even_re, even_im, odd_re, odd_im)
        forward(2 * p + 1, odd_re, odd_im, even_re, even_im)
        return carry

    lax.fori_loop(0, rotations // 2, rotation_pair, 0)
    if rotations % 2:
        forward(rotations - 1, even_re, even_im, odd_re, odd_im)
    for r in range(max(rotations - 2, 0), rotations):
        release(r)

    def drain(r, carry):
        for k in range(len(peers)):
            own_copy(r, k).wait_send()
        for k in range(len(far)):
            relay_copy(r, k).wait_send()
        for s in range(groups - 1):
            send_all(r, s).wait_recv()
        return carry

    lax.fori_loop(0, rotations, drain, 0)


def final_kernel(groups, planes, length, width, terms, blocks_ref, ty_ref, tz_ref, out_ref, low_ref, h_re, h_im):
    for s in range(groups):
        code = blocks_ref[0, s, planes].astype(jnp.int32).astype(F32)[:, :length]
        scale = jnp.exp2(code * (1.0 / LEVELS)) * (1.0 / TOP)
        parts = [blocks_ref[0, s, k].astype(jnp.int32).astype(F32) * scale[:, k : k + 1] for k in range(planes)]
        upper, lower = split(jnp.concatenate(parts, axis=0))
        lines = mul(jnp.concatenate([upper, upper, lower], axis=1), ty_ref[...])
        at = pl.ds(s * planes * width, planes * width)
        h_re[at, :] = lines[:, :length]
        h_im[at, :] = lines[:, length:]
    if terms > groups * planes:
        rest = pl.ds(groups * planes * width, (terms - groups * planes) * width)
        h_re[rest, :] = jnp.zeros(((terms - groups * planes) * width, length), F32)
        h_im[rest, :] = jnp.zeros(((terms - groups * planes) * width, length), F32)
    for i in range(0, width, 2):
        def both(ref):
            return split(jnp.concatenate([ref[pl.ds(i + t, terms, stride=width), :] for t in range(2)], axis=1))
        re_hi, re_lo = both(h_re)
        im_hi, im_lo = both(h_im)
        right = jnp.concatenate([re_hi, im_hi, re_lo, im_lo, re_hi, im_hi], axis=0)
        field = mul(tz_ref[...], right)
        for t in range(2):
            plane = field[:, t * length : (t + 1) * length]
            low_ref[0, 0, i + t : i + t + 1, :] = jnp.min(plane, axis=0, keepdims=True)
            out_ref[0, i + t] = plane.T


def best_kernel(groups, rotations, lows_ref, out_ref, held, send_sem, recv_sem):
    me = lax.axis_index("fft")
    others = [lax.rem(me + s, groups) for s in range(1, groups)]
    barrier = pltpu.get_barrier_semaphore()
    for peer in others:
        pl.semaphore_signal(barrier, inc=1, device_id={"fft": peer}, device_id_type=pl.DeviceIdType.MESH)
    held[me] = jnp.min(lows_ref[...], axis=(1, 2))
    pl.semaphore_wait(barrier, groups - 1)

    def share(s):
        return pltpu.make_async_remote_copy(
            src_ref=held.at[me], dst_ref=held.at[me], send_sem=send_sem.at[s], recv_sem=recv_sem.at[me],
            device_id={"fft": others[s]}, device_id_type=pl.DeviceIdType.MESH)

    def arrival(s):
        return pltpu.make_async_remote_copy(
            src_ref=held.at[me], dst_ref=held.at[others[s]], send_sem=send_sem.at[s], recv_sem=recv_sem.at[others[s]],
            device_id={"fft": others[s]}, device_id_type=pl.DeviceIdType.MESH)

    for s in range(groups - 1):
        share(s).start()
    for s in range(groups - 1):
        arrival(s).wait_recv()
        share(s).wait_send()
    low = jnp.min(jnp.min(held[...], axis=0), axis=1, keepdims=True)
    lane = lax.broadcasted_iota(jnp.int32, (rotations, 128), 1)
    row = lax.broadcasted_iota(jnp.int32, (rotations, 128), 0)
    out_ref[...] = jnp.sum(jnp.where(lane == row, low, 0.0), axis=0, keepdims=True)[:, :rotations]


def shards(receptor, ligand_grids, rot_index):
    groups = lax.axis_size("fft")
    channels, slab, length = receptor.shape[1], receptor.shape[2], receptor.shape[3]
    depth = ligand_grids.shape[2]
    box = depth * groups
    cells = ligand_grids.shape[3]
    rotations = rot_index.shape[0]
    xs = length // groups
    planes = slab // 2 + 1
    middle = (channels + 1) // 2
    cuts = tuple((start, stop, up((stop - start) * depth, 16)) for start, stop in ((0, middle), (middle, channels)))
    block = cuts[0][2] + cuts[1][2]
    top = up(planes * middle, 8)
    rows = up(top + planes * (channels - middle), 16)
    tops = (top, rows - top)
    freq = np.arange(length)

    t_z = []
    for (start, stop, size), top in zip(cuts, tops):
        table = np.zeros((groups, 2, top, groups, size))
        for d in range(groups):
            cz, sz = trig(d * slab + np.arange(planes), np.arange(box), length)
            for c in range(stop - start):
                at = np.arange(planes) * (stop - start) + c
                for s in range(groups):
                    span = slice(c * depth, (c + 1) * depth)
                    cut = slice(s * depth, (s + 1) * depth)
                    table[d, 0, at, s, span] = cz[:, cut]
                    table[d, 1, at, s, span] = -sz[:, cut]
        table = table.reshape(groups, 2 * top, groups * size)
        t_z.append(jnp.asarray(np.stack(halves(table), axis=1)))

    cy, sy = trig(np.arange(box), freq, length)
    per = 128 // box
    hi, lo = halves(np.concatenate([cy, -sy], axis=1)), halves(np.concatenate([sy, cy], axis=1))
    w_y = np.zeros((per, 512, 2 * length), ml_dtypes.bfloat16)
    for i in range(per):
        for part, (upper, lower) in enumerate((hi, lo)):
            for spot in (i * box, (i * box + 64) % 128):
                w_y[i, part * 128 + spot : part * 128 + spot + box] = upper
            w_y[i, 256 + part * 128 + i * box : 256 + part * 128 + (i + 1) * box] = lower
    w_y = jnp.asarray(w_y)

    t_x = np.block([[cy.T, sy.T], [-sy.T, cy.T]])
    hi, lo = halves(t_x)
    t_x = jnp.asarray(np.concatenate([hi, hi, lo], axis=1))

    cf, sf = trig(freq, freq, length)
    hi, lo = halves(np.concatenate([cf, sf], axis=1))
    t_i = jnp.asarray(np.concatenate([hi, lo, hi], axis=1))

    terms = up(groups * planes, 16)
    kz = np.zeros(terms, np.int64)
    weight = np.zeros(terms)
    for d in range(groups):
        for k in range(planes):
            f = d * slab + k
            kz[d * planes + k] = f
            if d < groups // 2:
                used = k < slab // 2
            else:
                used = k > 0 or f == length // 2
            weight[d * planes + k] = 0.0 if not used else 1.0 if f in (0, length // 2) else 2.0
    cb, sb = trig(freq, kz, length)
    hi, lo = halves(np.concatenate([cb * weight, -sb * weight], axis=1))
    t_b = jnp.asarray(np.concatenate([hi, hi, lo], axis=1))
    hi, lo = halves(np.block([[cf, sf], [-sf, cf]]) / float(length) ** 3)
    t_w = jnp.asarray(np.concatenate([hi, lo, hi], axis=0))

    own = pl.pallas_call(
        functools.partial(pick_kernel, cuts),
        grid_spec=pltpu.PrefetchScalarGridSpec(
            num_scalar_prefetch=1,
            grid=(rotations,),
            in_specs=[pl.BlockSpec((1, channels, depth, cells), lambda r, index: (index[r], 0, 0, 0))],
            out_specs=pl.BlockSpec((1, block, cells), lambda r, index: (r, 0, 0)),
        ),
        out_shape=jax.ShapeDtypeStruct((rotations, block, cells), BF),
    )(rot_index, ligand_grids)

    any_space = pl.BlockSpec(memory_space=pl.ANY)
    vmem = pl.BlockSpec(memory_space=pltpu.VMEM)
    sent = pl.pallas_call(
        functools.partial(main_kernel, channels, planes, box, groups, rotations, length, cuts, tops),
        in_specs=[any_space, any_space, any_space, any_space, vmem, vmem, vmem],
        out_specs=any_space,
        out_shape=jax.ShapeDtypeStruct((rotations, groups, planes + 1, xs, 2 * length), jnp.int16),
        scratch_shapes=[
            pltpu.VMEM((2, channels, planes, length, length), F32),
            pltpu.VMEM((2, 2, channels, length, length), BF),
            pltpu.VMEM((rotations, groups * block, cells), BF),
            pltpu.VMEM(t_z[0].shape[1:], BF),
            pltpu.VMEM(t_z[1].shape[1:], BF),
            pltpu.VMEM((2 * rows, cells), F32),
            pltpu.VMEM((rows * box, length), F32),
            pltpu.VMEM((rows * box, length), F32),
            pltpu.VMEM((rows * box, length), F32),
            pltpu.VMEM((rows * box, length), F32),
            pltpu.VMEM((-(-channels // 2), 2 * length, 2 * length), F32),
            pltpu.VMEM((-(-channels // 2), 2 * length, 2 * length), F32),
            pltpu.VMEM((2, 2 * length, 2 * length), BF),
            pltpu.VMEM((2, 2 * length, 2 * length), BF),
            pltpu.VMEM((length, length), F32),
            pltpu.VMEM((2, planes + 1, groups, xs, 2 * length), jnp.int16),
            pltpu.SemaphoreType.DMA((4,)),
            pltpu.SemaphoreType.DMA((rotations,)),
            pltpu.SemaphoreType.DMA((rotations, groups)),
            pltpu.SemaphoreType.DMA((rotations, groups)),
            pltpu.SemaphoreType.DMA((rotations, groups)),
            pltpu.SemaphoreType.DMA((rotations, groups)),
            pltpu.SemaphoreType.DMA((rotations,)),
        ],
        compiler_params=pltpu.CompilerParams(
            collective_id=0, has_side_effects=True, vmem_limit_bytes=60 * 2**20),
        cost_estimate=pl.CostEstimate(flops=rotations * 6 * 10**9, bytes_accessed=30_000_000, transcendentals=0),
    )(receptor, own, *t_z, w_y, t_x, t_i)

    width = min(16, xs)
    scores, lows = pl.pallas_call(
        functools.partial(final_kernel, groups, planes, length, width, terms),
        grid=(rotations, xs // width),
        in_specs=[
            pl.BlockSpec((1, groups, planes + 1, width, 2 * length), lambda r, x: (r, 0, 0, x, 0)),
            pl.BlockSpec(t_w.shape, lambda r, x: (0, 0)),
            pl.BlockSpec(t_b.shape, lambda r, x: (0, 0)),
        ],
        out_specs=[
            pl.BlockSpec((1, width, length, length), lambda r, x: (r, x, 0, 0)),
            pl.BlockSpec((1, 1, width, length), lambda r, x: (r, x, 0, 0)),
        ],
        out_shape=[
            jax.ShapeDtypeStruct((rotations, xs, length, length), F32),
            jax.ShapeDtypeStruct((rotations, xs // width, width, length), F32),
        ],
        scratch_shapes=[pltpu.VMEM((terms * width, length), F32)] * 2,
        compiler_params=pltpu.CompilerParams(vmem_limit_bytes=60 * 2**20),
        cost_estimate=pl.CostEstimate(flops=rotations * 10**9, bytes_accessed=20_000_000, transcendentals=0),
    )(sent, t_w, t_b)
    best = pl.pallas_call(
        functools.partial(best_kernel, groups, rotations),
        in_specs=[vmem],
        out_specs=vmem,
        out_shape=jax.ShapeDtypeStruct((1, rotations), F32),
        scratch_shapes=[
            pltpu.VMEM((groups, rotations, length), F32),
            pltpu.SemaphoreType.DMA((groups,)),
            pltpu.SemaphoreType.DMA((groups,)),
        ],
        compiler_params=pltpu.CompilerParams(collective_id=1, has_side_effects=True),
    )(lows)
    return scores, best.reshape(rotations)


def solution(mesh):
    placed = (P(None, None, "fft", None, None), P(None, None, "fft", None), P("rot"))
    return jax.shard_map(
        shards,
        mesh=mesh,
        in_specs=placed,
        out_specs=(P("rot", "fft", None, None), P("rot")),
        check_vma=False,
    )
```

```python
import functools
import math

import jax
import jax.numpy as jnp
import ml_dtypes
import numpy as np
from jax import lax
from jax.experimental import pallas as pl
from jax.experimental.pallas import tpu as pltpu
from jax.sharding import PartitionSpec as P

BF = jnp.bfloat16
F32 = jnp.float32
TOP = 32767.0
LEVELS = 256.0


def halves(table):
    upper = table.astype(np.float32).astype(ml_dtypes.bfloat16)
    lower = (table - upper.astype(np.float64)).astype(np.float32)
    return upper, lower.astype(ml_dtypes.bfloat16)


def trig(rows, cols, length):
    angle = (np.outer(rows, cols) % length) * (2.0 * math.pi / length)
    return np.cos(angle), np.sin(angle)


def split(values):
    upper = values.astype(BF)
    return upper, (values - upper.astype(F32)).astype(BF)


def mul(left, right):
    return jnp.dot(left, right, preferred_element_type=F32)


def mul_t(left, right):
    return lax.dot_general(left, right, (((1,), (1,)), ((), ())), preferred_element_type=F32)


def up(value, step):
    return -(-value // step) * step


def pick_kernel(cuts, index_ref, in_ref, out_ref):
    depth, cells = in_ref.shape[2], in_ref.shape[3]
    parts = []
    for start, stop, size in cuts:
        parts += [in_ref[0, c].astype(F32) for c in range(start, stop)]
        if size > (stop - start) * depth:
            parts.append(jnp.zeros((size - (stop - start) * depth, cells), F32))
    out_ref[0] = jnp.concatenate(parts, axis=0).astype(BF)


def main_kernel(
    channels, planes, box, groups, rotations, length, cuts, tops, width, terms,
    rec_hbm, own_hbm, tza_hbm, tzb_hbm, wy_ref, tx_ref, ti_ref, ty_ref, tb_ref, recv_hbm, early_hbm, low_ref,
    rec, stage, lbuf, tza, tzb, a_buf, even_re, even_im, odd_re, odd_im, spec_a, spec_b, square_a, square_b, expo, qbuf, blocks, ready, h_re, h_im,
    load_sem, own_sem, gsend, grecv, xsend, xrecv, self_sem, in_sem, out_sem,
):
    me = lax.axis_index("fft")
    block = cuts[0][2] + cuts[1][2]
    rows = tops[0] + tops[1]
    middle = cuts[1][0]
    xs = length // groups
    sib = me + 1 - 2 * lax.rem(me, 2)
    far = [lax.rem(me + 2 * m, groups) for m in range(1, groups // 2)]
    peers = [sib] + far
    others = [lax.rem(me + s, groups) for s in range(1, groups)]
    pairs = -(-channels // 2)

    def fetch(k):
        slot_at = lax.rem(k, 2)
        return pltpu.make_async_copy(rec_hbm.at[:, :, k], stage.at[slot_at], load_sem.at[slot_at])

    fetch(0).start()
    table_copies = [
        pltpu.make_async_copy(tza_hbm.at[me], tza, load_sem.at[2]),
        pltpu.make_async_copy(tzb_hbm.at[me], tzb, load_sem.at[3]),
    ]
    for copy in table_copies:
        copy.start()

    barrier = pltpu.get_barrier_semaphore()
    for peer in others:
        pl.semaphore_signal(barrier, inc=1, device_id={"fft": peer}, device_id_type=pl.DeviceIdType.MESH)
    pl.semaphore_wait(barrier, groups - 1)

    def slot(r, source):
        return lbuf.at[r, pl.ds(pl.multiple_of(source * block, block), block)]

    def own_copy(r, k):
        return pltpu.make_async_remote_copy(
            src_ref=own_hbm.at[r], dst_ref=slot(r, me), send_sem=gsend.at[r, k], recv_sem=grecv.at[r, me],
            device_id={"fft": peers[k]}, device_id_type=pl.DeviceIdType.MESH)

    def relay_copy(r, k):
        return pltpu.make_async_remote_copy(
            src_ref=slot(r, far[k]), dst_ref=slot(r, far[k]), send_sem=gsend.at[r, len(peers) + k],
            recv_sem=grecv.at[r, far[k]], device_id={"fft": sib}, device_id_type=pl.DeviceIdType.MESH)

    def arrival(r, source):
        return pltpu.make_async_remote_copy(
            src_ref=own_hbm.at[r], dst_ref=slot(r, source), send_sem=gsend.at[r, 0], recv_sem=grecv.at[r, source],
            device_id={"fft": sib}, device_id_type=pl.DeviceIdType.MESH)

    def local(r):
        return pltpu.make_async_copy(own_hbm.at[r], slot(r, me), own_sem.at[r])

    def begin(r):
        for k in range(len(peers)):
            own_copy(r, k).start()
        local(r).start()

    def relay(r):
        for k in range(len(far)):
            arrival(r, far[k]).wait_recv()
            relay_copy(r, k).start()

    def finish(r):
        arrival(r, sib).wait_recv()
        for m in range(1, groups // 2):
            arrival(r, lax.rem(sib + 2 * m, groups)).wait_recv()
        local(r).wait()

    def send_plane(r, k, s):
        peer = others[s]
        return pltpu.make_async_remote_copy(
            src_ref=qbuf.at[lax.rem(r, 2), k, peer], dst_ref=recv_hbm.at[r, me, k],
            send_sem=xsend.at[r, s], recv_sem=xrecv.at[r, me],
            device_id={"fft": peer}, device_id_type=pl.DeviceIdType.MESH)

    def send_all(r, s):
        peer = others[s]
        return pltpu.make_async_remote_copy(
            src_ref=qbuf.at[lax.rem(r, 2), :, peer], dst_ref=recv_hbm.at[r, peer],
            send_sem=xsend.at[r, s], recv_sem=xrecv.at[r, peer],
            device_id={"fft": peer}, device_id_type=pl.DeviceIdType.MESH)

    def keep(r):
        return pltpu.make_async_copy(
            qbuf.at[lax.rem(r, 2), :, me], recv_hbm.at[r, me], self_sem.at[r])

    lanes = lax.broadcasted_iota(jnp.int32, (length, length), 1)

    per = 128 // box
    lane_groups = box * box // 128

    def z_stage(r):
        for half, table in enumerate((tza, tzb)):
            skip, size, top = half * cuts[0][2], cuts[half][2], tops[half]
            cells = jnp.concatenate([lbuf[r, s * block + skip : s * block + skip + size] for s in range(groups)], axis=0)
            out = mul(table[0], cells) + mul(table[1], cells)
            to = half * tops[0]
            a_buf[to : to + top] = out[:top]
            a_buf[rows + to : rows + to + top] = out[top:]

    first_lanes = lax.broadcasted_iota(jnp.int32, (rows, 128), 1) < 64

    def lane_group(j, b_re, b_im):
        at = pl.ds(pl.multiple_of(j * 128, 128), 128)
        whole, early, late = [], [], []
        for values in (a_buf[0:rows, at], a_buf[rows : 2 * rows, at]):
            upper = values.astype(BF)
            wide = upper.astype(F32)
            lower = pltpu.roll(values - wide, 64, 1)
            whole.append(upper)
            early.append(jnp.where(first_lanes, wide, lower).astype(BF))
            late.append(jnp.where(first_lanes, lower, wide).astype(BF))
        for i in range(per):
            out = mul(jnp.concatenate((early if i < per // 2 else late) + whole, axis=1), wy_ref[i])
            for g in range(rows // 8):
                to = pl.ds(pl.multiple_of((g * box + j * per + i) * 8, 8), 8)
                b_re[to, :] = out[g * 8 : g * 8 + 8, :length]
                b_im[to, :] = out[g * 8 : g * 8 + 8, length:]

    def release(r):
        for s in range(groups - 1):
            send_all(r, s).wait_send()
        keep(r).wait()

    def forward(r, b_re, b_im, next_re, next_im):
        q = lax.rem(r, 2)

        @pl.when(r + 1 < rotations)
        def _():
            finish(r + 1)

        z_stage(jnp.minimum(r + 1, rotations - 1))

        @pl.when(r + 2 < rotations)
        def _():
            relay(r + 2)

        @pl.when(r + 3 < rotations)
        def _():
            begin(r + 3)

        @pl.when(r >= 2)
        def _():
            release(r - 2)

        def x_stage(k, spec):
            for p in range(pairs):
                pair = range(2 * p, min(2 * p + 2, channels))
                def pick(ref):
                    parts = []
                    for c in pair:
                        row = k * middle + c if c < middle else tops[0] + k * (channels - middle) + c - middle
                        parts.append(ref[pl.ds(row // 8 * (box * 8) + lax.rem(row, 8), box, stride=8), :])
                    return split(jnp.concatenate(parts, axis=1))
                re_hi, re_lo = pick(b_re)
                im_hi, im_lo = pick(b_im)
                right = jnp.concatenate([re_hi, im_hi, re_lo, im_lo, re_hi, im_hi], axis=0)
                spec[p, :, 0 : length * len(pair)] = mul(tx_ref[...], right)

        def product(k, spec, square):
            for h in range(0, length, 16):
                low, high = slice(h, h + 16), slice(length + h, length + h + 16)
                p_re = p_im = None
                for c in range(channels):
                    at = slice((c % 2) * length, (c % 2 + 1) * length)
                    s_re = spec[c // 2, low, at]
                    s_im = spec[c // 2, high, at]
                    r_re = rec[0, c, k, low]
                    r_im = rec[1, c, k, low]
                    q_re = r_re * s_re + r_im * s_im
                    q_im = r_im * s_re - r_re * s_im
                    p_re = q_re if p_re is None else p_re + q_re
                    p_im = q_im if p_im is None else p_im + q_im
                for t, (re, im) in enumerate(zip(split(p_re), split(p_im))):
                    square[t, low, 0:length] = re
                    square[t, low, length : 2 * length] = im
                    square[t, high, 0:length] = -im
                    square[t, high, length : 2 * length] = re

        def close(k, square):
            upper = square[0]
            field = mul(ti_ref[...], jnp.concatenate([upper, upper, square[1]], axis=0))
            most = jnp.max(jnp.abs(field), axis=1, keepdims=True)
            code = jnp.ceil(LEVELS * jnp.log2(jnp.maximum(most, 1e-30))) + 1.0
            factor = TOP * jnp.exp2(code * (-1.0 / LEVELS))
            qbuf[q, k] = jnp.round(field * factor).astype(jnp.int32).reshape(groups, xs, 2 * length).astype(jnp.int16)
            expo[...] = jnp.where(lanes == k, code, expo[...])

        def send(k):
            for s in range(groups - 1):
                send_plane(r, k, s).start()

        each = -(-lane_groups // (planes // 2))

        def two(m, carry):
            k = 2 * m
            x_stage(k - 1, spec_b)
            for g in range(each):
                lane_group(jnp.minimum((m - 1) * each + g, lane_groups - 1), next_re, next_im)
            product(k - 2, spec_a, square_a)
            close(jnp.maximum(k - 3, 0), square_b)
            x_stage(k, spec_a)
            product(k - 1, spec_b, square_b)
            close(k - 2, square_a)

            @pl.when(m > 1)
            def _():
                send(k - 3)

            send(k - 2)
            return carry

        x_stage(0, spec_a)
        lax.fori_loop(1, planes // 2 + 1, two, 0)
        product(planes - 1, spec_a, square_a)
        close(planes - 2, square_b)
        close(planes - 1, square_a)
        send(planes - 2)
        send(planes - 1)
        codes = expo[...].astype(jnp.int32)
        codes = jnp.concatenate([codes, codes], axis=1)
        qbuf[q, planes] = codes.reshape(groups, xs, 2 * length).astype(jnp.int16)
        send(planes)
        keep(r).start()

    for r in range(min(3, rotations)):
        begin(r)

    def widen(k, carry):
        @pl.when(k + 1 < planes)
        def _():
            fetch(k + 1).start()

        fetch(k).wait()
        for part in range(2):
            for c in range(channels):
                rec[part, c, k] = stage[lax.rem(k, 2), part, c].astype(F32)
        return carry

    lax.fori_loop(0, planes, widen, 0)
    for copy in table_copies:
        copy.wait()
    relay(0)
    finish(0)
    z_stage(0)
    if rotations > 1:
        relay(1)

    def first(j, carry):
        lane_group(j, even_re, even_im)
        return carry

    lax.fori_loop(0, lane_groups, first, 0)

    parts = xs // width

    def load_block(f, h):
        return pltpu.make_async_copy(recv_hbm.at[f, :, :, pl.ds(h * width, width)], blocks.at[h], in_sem.at[h])

    def store_block(f, h):
        return pltpu.make_async_copy(ready.at[h], early_hbm.at[f, pl.ds(h * width, width)], out_sem.at[h])

    def end(f, carry):
        for s in range(groups - 1):
            send_all(f, s).wait_recv()
        for h in range(parts):
            load_block(f, h).start()
        for h in range(parts):
            @pl.when(f > 0)
            def _():
                store_block(f - 1, h).wait()

            load_block(f, h).wait()
            end_block(
                groups, planes, length, width, terms, lambda s, k: blocks[h, s, k], ty_ref, tb_ref,
                ready.at[h], low_ref.at[f, h], h_re, h_im)
            store_block(f, h).start()
        return carry

    def rotation_pair(p, carry):
        forward(2 * p, even_re, even_im, odd_re, odd_im)
        forward(2 * p + 1, odd_re, odd_im, even_re, even_im)
        lax.fori_loop(jnp.maximum(2 * p - 2, 0), 2 * p, end, 0)
        return carry

    lax.fori_loop(0, rotations // 2, rotation_pair, 0)
    if rotations % 2:
        forward(rotations - 1, even_re, even_im, odd_re, odd_im)
    for r in range(max(rotations - 2, 0), rotations):
        release(r)
    early = 2 * (rotations // 2) - 2
    for h in range(parts):
        store_block(early - 1, h).wait()

    def drain(r, carry):
        for k in range(len(peers)):
            own_copy(r, k).wait_send()
        for k in range(len(far)):
            relay_copy(r, k).wait_send()
        @pl.when(r >= early)
        def _():
            for s in range(groups - 1):
                send_all(r, s).wait_recv()

        return carry

    lax.fori_loop(0, rotations, drain, 0)


def end_block(groups, planes, length, width, terms, read, ty_ref, tz_ref, out_ref, low_ref, h_re, h_im):
    for s in range(groups):
        code = read(s, planes).astype(jnp.int32).astype(F32)[:, :length]
        scale = jnp.exp2(code * (1.0 / LEVELS)) * (1.0 / TOP)
        parts = [read(s, k).astype(jnp.int32).astype(F32) * scale[:, k : k + 1] for k in range(planes)]
        upper, lower = split(jnp.concatenate(parts, axis=0))
        lines = mul(jnp.concatenate([upper, upper, lower], axis=1), ty_ref[...])
        at = pl.ds(s * planes * width, planes * width)
        h_re[at, :] = lines[:, :length]
        h_im[at, :] = lines[:, length:]
    if terms > groups * planes:
        rest = pl.ds(groups * planes * width, (terms - groups * planes) * width)
        h_re[rest, :] = jnp.zeros(((terms - groups * planes) * width, length), F32)
        h_im[rest, :] = jnp.zeros(((terms - groups * planes) * width, length), F32)
    for i in range(0, width, 2):
        def both(ref):
            return split(jnp.concatenate([ref[pl.ds(i + t, terms, stride=width), :] for t in range(2)], axis=1))
        re_hi, re_lo = both(h_re)
        im_hi, im_lo = both(h_im)
        right = jnp.concatenate([re_hi, im_hi, re_lo, im_lo, re_hi, im_hi], axis=0)
        field = mul(tz_ref[...], right)
        for t in range(2):
            plane = field[:, t * length : (t + 1) * length]
            low_ref[i + t : i + t + 1, :] = jnp.min(plane, axis=0, keepdims=True)
            out_ref[i + t] = plane.T


def final_kernel(
    groups, planes, length, width, terms, early, parts, steps,
    blocks_ref, early_hbm, ty_ref, tz_ref, out_hbm, low_ref, ready, h_re, h_im, hold, copy_sem, out_sem,
):
    step = pl.program_id(0) * parts + pl.program_id(1)

    def store_block(t):
        at = pl.ds(pl.multiple_of(lax.rem(t, parts) * width, width), width)
        return pltpu.make_async_copy(ready.at[lax.rem(t, 2)], out_hbm.at[early + t // parts, at], out_sem.at[lax.rem(t, 2)])

    def bring(r):
        return pltpu.make_async_copy(early_hbm.at[r], hold.at[r], copy_sem.at[0, r])

    def hand(r):
        return pltpu.make_async_copy(hold.at[r], out_hbm.at[r], copy_sem.at[1, r])

    @pl.when(step == 0)
    def _():
        for r in range(early):
            bring(r).start()

    @pl.when(step >= 2)
    def _():
        store_block(step - 2).wait()

    end_block(
        groups, planes, length, width, terms, lambda s, k: blocks_ref[0, s, k], ty_ref, tz_ref,
        ready.at[lax.rem(step, 2)], low_ref.at[0, 0], h_re, h_im)
    store_block(step).start()
    for r in range(early):
        @pl.when(step == r * steps // early)
        def _():
            bring(r).wait()
            hand(r).start()

    @pl.when(step == steps - 1)
    def _():
        if steps > 1:
            store_block(step - 1).wait()
        store_block(step).wait()
        for r in range(early):
            hand(r).wait()


def best_kernel(groups, rotations, early, first_ref, last_ref, out_ref, held, send_sem, recv_sem):
    me = lax.axis_index("fft")
    others = [lax.rem(me + s, groups) for s in range(1, groups)]
    barrier = pltpu.get_barrier_semaphore()
    for peer in others:
        pl.semaphore_signal(barrier, inc=1, device_id={"fft": peer}, device_id_type=pl.DeviceIdType.MESH)
    held[me, 0:early] = jnp.min(first_ref[...], axis=(1, 2))
    held[me, early:rotations] = jnp.min(last_ref[...], axis=(1, 2))
    pl.semaphore_wait(barrier, groups - 1)

    def share(s):
        return pltpu.make_async_remote_copy(
            src_ref=held.at[me], dst_ref=held.at[me], send_sem=send_sem.at[s], recv_sem=recv_sem.at[me],
            device_id={"fft": others[s]}, device_id_type=pl.DeviceIdType.MESH)

    def arrival(s):
        return pltpu.make_async_remote_copy(
            src_ref=held.at[me], dst_ref=held.at[others[s]], send_sem=send_sem.at[s], recv_sem=recv_sem.at[others[s]],
            device_id={"fft": others[s]}, device_id_type=pl.DeviceIdType.MESH)

    for s in range(groups - 1):
        share(s).start()
    for s in range(groups - 1):
        arrival(s).wait_recv()
        share(s).wait_send()
    low = jnp.min(jnp.min(held[...], axis=0), axis=1, keepdims=True)
    lane = lax.broadcasted_iota(jnp.int32, (rotations, 128), 1)
    row = lax.broadcasted_iota(jnp.int32, (rotations, 128), 0)
    out_ref[...] = jnp.sum(jnp.where(lane == row, low, 0.0), axis=0, keepdims=True)[:, :rotations]


def shards(receptor, ligand_grids, rot_index):
    groups = lax.axis_size("fft")
    channels, slab, length = receptor.shape[1], receptor.shape[2], receptor.shape[3]
    depth = ligand_grids.shape[2]
    box = depth * groups
    cells = ligand_grids.shape[3]
    rotations = rot_index.shape[0]
    xs = length // groups
    planes = slab // 2 + 1
    middle = (channels + 1) // 2
    cuts = tuple((start, stop, up((stop - start) * depth, 16)) for start, stop in ((0, middle), (middle, channels)))
    block = cuts[0][2] + cuts[1][2]
    top = up(planes * middle, 8)
    rows = up(top + planes * (channels - middle), 16)
    tops = (top, rows - top)
    freq = np.arange(length)

    t_z = []
    for (start, stop, size), top in zip(cuts, tops):
        table = np.zeros((groups, 2, top, groups, size))
        for d in range(groups):
            cz, sz = trig(d * slab + np.arange(planes), np.arange(box), length)
            for c in range(stop - start):
                at = np.arange(planes) * (stop - start) + c
                for s in range(groups):
                    span = slice(c * depth, (c + 1) * depth)
                    cut = slice(s * depth, (s + 1) * depth)
                    table[d, 0, at, s, span] = cz[:, cut]
                    table[d, 1, at, s, span] = -sz[:, cut]
        table = table.reshape(groups, 2 * top, groups * size)
        t_z.append(jnp.asarray(np.stack(halves(table), axis=1)))

    cy, sy = trig(np.arange(box), freq, length)
    per = 128 // box
    hi, lo = halves(np.concatenate([cy, -sy], axis=1)), halves(np.concatenate([sy, cy], axis=1))
    w_y = np.zeros((per, 512, 2 * length), ml_dtypes.bfloat16)
    for i in range(per):
        for part, (upper, lower) in enumerate((hi, lo)):
            for spot in (i * box, (i * box + 64) % 128):
                w_y[i, part * 128 + spot : part * 128 + spot + box] = upper
            w_y[i, 256 + part * 128 + i * box : 256 + part * 128 + (i + 1) * box] = lower
    w_y = jnp.asarray(w_y)

    t_x = np.block([[cy.T, sy.T], [-sy.T, cy.T]])
    hi, lo = halves(t_x)
    t_x = jnp.asarray(np.concatenate([hi, hi, lo], axis=1))

    cf, sf = trig(freq, freq, length)
    hi, lo = halves(np.concatenate([cf, sf], axis=1))
    t_i = jnp.asarray(np.concatenate([hi, lo, hi], axis=1))

    terms = up(groups * planes, 16)
    kz = np.zeros(terms, np.int64)
    weight = np.zeros(terms)
    for d in range(groups):
        for k in range(planes):
            f = d * slab + k
            kz[d * planes + k] = f
            if d < groups // 2:
                used = k < slab // 2
            else:
                used = k > 0 or f == length // 2
            weight[d * planes + k] = 0.0 if not used else 1.0 if f in (0, length // 2) else 2.0
    cb, sb = trig(freq, kz, length)
    hi, lo = halves(np.concatenate([cb * weight, -sb * weight], axis=1))
    t_b = jnp.asarray(np.concatenate([hi, hi, lo], axis=1))
    hi, lo = halves(np.block([[cf, sf], [-sf, cf]]) / float(length) ** 3)
    t_w = jnp.asarray(np.concatenate([hi, lo, hi], axis=0))

    own = pl.pallas_call(
        functools.partial(pick_kernel, cuts),
        grid_spec=pltpu.PrefetchScalarGridSpec(
            num_scalar_prefetch=1,
            grid=(rotations,),
            in_specs=[pl.BlockSpec((1, channels, depth, cells), lambda r, index: (index[r], 0, 0, 0))],
            out_specs=pl.BlockSpec((1, block, cells), lambda r, index: (r, 0, 0)),
        ),
        out_shape=jax.ShapeDtypeStruct((rotations, block, cells), BF),
    )(rot_index, ligand_grids)

    any_space = pl.BlockSpec(memory_space=pl.ANY)
    vmem = pl.BlockSpec(memory_space=pltpu.VMEM)
    width = min(16, xs)
    parts = xs // width
    early = 2 * (rotations // 2) - 2
    late = rotations - early
    sent, early_scores, early_lows = pl.pallas_call(
        functools.partial(main_kernel, channels, planes, box, groups, rotations, length, cuts, tops, width, terms),
        in_specs=[any_space] * 4 + [vmem] * 5,
        out_specs=[any_space, any_space, vmem],
        out_shape=[
            jax.ShapeDtypeStruct((rotations, groups, planes + 1, xs, 2 * length), jnp.int16),
            jax.ShapeDtypeStruct((early, xs, length, length), F32),
            jax.ShapeDtypeStruct((early, parts, width, length), F32),
        ],
        scratch_shapes=[
            pltpu.VMEM((2, channels, planes, length, length), F32),
            pltpu.VMEM((2, 2, channels, length, length), BF),
            pltpu.VMEM((rotations, groups * block, cells), BF),
            pltpu.VMEM(t_z[0].shape[1:], BF),
            pltpu.VMEM(t_z[1].shape[1:], BF),
            pltpu.VMEM((2 * rows, cells), F32),
            pltpu.VMEM((rows * box, length), F32),
            pltpu.VMEM((rows * box, length), F32),
            pltpu.VMEM((rows * box, length), F32),
            pltpu.VMEM((rows * box, length), F32),
            pltpu.VMEM((-(-channels // 2), 2 * length, 2 * length), F32),
            pltpu.VMEM((-(-channels // 2), 2 * length, 2 * length), F32),
            pltpu.VMEM((2, 2 * length, 2 * length), BF),
            pltpu.VMEM((2, 2 * length, 2 * length), BF),
            pltpu.VMEM((length, length), F32),
            pltpu.VMEM((2, planes + 1, groups, xs, 2 * length), jnp.int16),
            pltpu.VMEM((parts, groups, planes + 1, width, 2 * length), jnp.int16),
            pltpu.VMEM((parts, width, length, length), F32),
            pltpu.VMEM((terms * width, length), F32),
            pltpu.VMEM((terms * width, length), F32),
            pltpu.SemaphoreType.DMA((4,)),
            pltpu.SemaphoreType.DMA((rotations,)),
            pltpu.SemaphoreType.DMA((rotations, groups)),
            pltpu.SemaphoreType.DMA((rotations, groups)),
            pltpu.SemaphoreType.DMA((rotations, groups)),
            pltpu.SemaphoreType.DMA((rotations, groups)),
            pltpu.SemaphoreType.DMA((rotations,)),
            pltpu.SemaphoreType.DMA((parts,)),
            pltpu.SemaphoreType.DMA((parts,)),
        ],
        compiler_params=pltpu.CompilerParams(
            collective_id=0, has_side_effects=True, vmem_limit_bytes=60 * 2**20),
        cost_estimate=pl.CostEstimate(flops=rotations * 6 * 10**9, bytes_accessed=30_000_000, transcendentals=0),
    )(receptor, own, *t_z, w_y, t_x, t_i, t_w, t_b)

    scores, late_lows = pl.pallas_call(
        functools.partial(final_kernel, groups, planes, length, width, terms, early, parts, late * parts),
        grid=(late, parts),
        in_specs=[
            pl.BlockSpec((1, groups, planes + 1, width, 2 * length), lambda r, x: (early + r, 0, 0, x, 0)),
            any_space,
            pl.BlockSpec(t_w.shape, lambda r, x: (0, 0)),
            pl.BlockSpec(t_b.shape, lambda r, x: (0, 0)),
        ],
        out_specs=[any_space, pl.BlockSpec((1, 1, width, length), lambda r, x: (r, x, 0, 0))],
        out_shape=[
            jax.ShapeDtypeStruct((rotations, xs, length, length), F32),
            jax.ShapeDtypeStruct((late, parts, width, length), F32),
        ],
        scratch_shapes=[
            pltpu.VMEM((2, width, length, length), F32),
            pltpu.VMEM((terms * width, length), F32),
            pltpu.VMEM((terms * width, length), F32),
            pltpu.VMEM((early, xs, length, length), F32),
            pltpu.SemaphoreType.DMA((2, early)),
            pltpu.SemaphoreType.DMA((2,)),
        ],
        compiler_params=pltpu.CompilerParams(vmem_limit_bytes=60 * 2**20),
        cost_estimate=pl.CostEstimate(flops=late * 10**9, bytes_accessed=20_000_000, transcendentals=0),
    )(sent, early_scores, t_w, t_b)
    best = pl.pallas_call(
        functools.partial(best_kernel, groups, rotations, early),
        in_specs=[vmem, vmem],
        out_specs=vmem,
        out_shape=jax.ShapeDtypeStruct((1, rotations), F32),
        scratch_shapes=[
            pltpu.VMEM((groups, rotations, length), F32),
            pltpu.SemaphoreType.DMA((groups,)),
            pltpu.SemaphoreType.DMA((groups,)),
        ],
        compiler_params=pltpu.CompilerParams(collective_id=1, has_side_effects=True),
    )(early_lows, late_lows)
    return scores, best.reshape(rotations)


def solution(mesh):
    placed = (P(None, None, "fft", None, None), P(None, None, "fft", None), P("rot"))
    return jax.shard_map(
        shards,
        mesh=mesh,
        in_specs=placed,
        out_specs=(P("rot", "fft", None, None), P("rot")),
        check_vma=False,
    )
```

```python
import functools
import math

import jax
import jax.numpy as jnp
import ml_dtypes
import numpy as np
from jax import lax
from jax.experimental import pallas as pl
from jax.experimental.pallas import tpu as pltpu
from jax.sharding import PartitionSpec as P

BF = jnp.bfloat16
F32 = jnp.float32
TOP = 32767.0
LEVELS = 256.0


def halves(table):
    upper = table.astype(np.float32).astype(ml_dtypes.bfloat16)
    lower = (table - upper.astype(np.float64)).astype(np.float32)
    return upper, lower.astype(ml_dtypes.bfloat16)


def trig(rows, cols, length):
    angle = (np.outer(rows, cols) % length) * (2.0 * math.pi / length)
    return np.cos(angle), np.sin(angle)


def split(values):
    upper = values.astype(BF)
    return upper, (values - upper.astype(F32)).astype(BF)


def mul(left, right):
    return jnp.dot(left, right, preferred_element_type=F32)


def mul_t(left, right):
    return lax.dot_general(left, right, (((1,), (1,)), ((), ())), preferred_element_type=F32)


def up(value, step):
    return -(-value // step) * step


def pick_kernel(cuts, index_ref, table_hbm, out_ref, held, sems):
    rotations, depth, cells = held.shape[0], held.shape[2], held.shape[3]

    def fetch(r):
        return pltpu.make_async_copy(table_hbm.at[index_ref[r]], held.at[r], sems.at[r])

    for r in range(rotations):
        fetch(r).start()
    for r in range(rotations):
        fetch(r).wait()
        parts = []
        for start, stop, size in cuts:
            parts += [held[r, c].astype(F32) for c in range(start, stop)]
            if size > (stop - start) * depth:
                parts.append(jnp.zeros((size - (stop - start) * depth, cells), F32))
        out_ref[r] = jnp.concatenate(parts, axis=0).astype(BF)


def main_kernel(
    channels, planes, box, groups, rotations, length, cuts, tops, width, terms,
    rec_hbm, own_hbm, tza_hbm, tzb_hbm, wy_ref, tx_ref, ti_ref, ty_ref, tb_ref, recv_hbm, early_hbm, low_ref,
    rec, stage, lbuf, tza, tzb, a_buf, even_re, even_im, odd_re, odd_im, spec_a, spec_b, square_a, square_b, expo, qbuf, blocks, ready, h_re, h_im,
    load_sem, own_sem, gsend, grecv, xsend, xrecv, self_sem, in_sem, out_sem,
):
    me = lax.axis_index("fft")
    block = cuts[0][2] + cuts[1][2]
    rows = tops[0] + tops[1]
    middle = cuts[1][0]
    xs = length // groups
    sib = me + 1 - 2 * lax.rem(me, 2)
    far = [lax.rem(me + 2 * m, groups) for m in range(1, groups // 2)]
    peers = [sib] + far
    others = [lax.rem(me + s, groups) for s in range(1, groups)]
    pairs = -(-channels // 2)

    def fetch(k):
        slot_at = lax.rem(k, 2)
        return pltpu.make_async_copy(rec_hbm.at[:, :, k], stage.at[slot_at], load_sem.at[slot_at])

    fetch(0).start()
    table_copies = [
        pltpu.make_async_copy(tza_hbm.at[me], tza, load_sem.at[2]),
        pltpu.make_async_copy(tzb_hbm.at[me], tzb, load_sem.at[3]),
    ]
    for copy in table_copies:
        copy.start()

    barrier = pltpu.get_barrier_semaphore()
    for peer in others:
        pl.semaphore_signal(barrier, inc=1, device_id={"fft": peer}, device_id_type=pl.DeviceIdType.MESH)
    pl.semaphore_wait(barrier, groups - 1)

    def slot(r, source):
        return lbuf.at[r, pl.ds(pl.multiple_of(source * block, block), block)]

    def own_copy(r, k):
        return pltpu.make_async_remote_copy(
            src_ref=own_hbm.at[r], dst_ref=slot(r, me), send_sem=gsend.at[r, k], recv_sem=grecv.at[r, me],
            device_id={"fft": peers[k]}, device_id_type=pl.DeviceIdType.MESH)

    def relay_copy(r, k):
        return pltpu.make_async_remote_copy(
            src_ref=slot(r, far[k]), dst_ref=slot(r, far[k]), send_sem=gsend.at[r, len(peers) + k],
            recv_sem=grecv.at[r, far[k]], device_id={"fft": sib}, device_id_type=pl.DeviceIdType.MESH)

    def arrival(r, source):
        return pltpu.make_async_remote_copy(
            src_ref=own_hbm.at[r], dst_ref=slot(r, source), send_sem=gsend.at[r, 0], recv_sem=grecv.at[r, source],
            device_id={"fft": sib}, device_id_type=pl.DeviceIdType.MESH)

    def local(r):
        return pltpu.make_async_copy(own_hbm.at[r], slot(r, me), own_sem.at[r])

    def begin(r):
        for k in range(len(peers)):
            own_copy(r, k).start()
        local(r).start()

    def relay(r):
        for k in range(len(far)):
            arrival(r, far[k]).wait_recv()
            relay_copy(r, k).start()

    def finish(r):
        arrival(r, sib).wait_recv()
        for m in range(1, groups // 2):
            arrival(r, lax.rem(sib + 2 * m, groups)).wait_recv()
        local(r).wait()

    def send_plane(r, k, s):
        peer = others[s]
        return pltpu.make_async_remote_copy(
            src_ref=qbuf.at[lax.rem(r, 2), k, peer], dst_ref=recv_hbm.at[r, me, k],
            send_sem=xsend.at[r, s], recv_sem=xrecv.at[r, me],
            device_id={"fft": peer}, device_id_type=pl.DeviceIdType.MESH)

    def send_all(r, s):
        peer = others[s]
        return pltpu.make_async_remote_copy(
            src_ref=qbuf.at[lax.rem(r, 2), :, peer], dst_ref=recv_hbm.at[r, peer],
            send_sem=xsend.at[r, s], recv_sem=xrecv.at[r, peer],
            device_id={"fft": peer}, device_id_type=pl.DeviceIdType.MESH)

    def keep(r):
        return pltpu.make_async_copy(
            qbuf.at[lax.rem(r, 2), :, me], recv_hbm.at[r, me], self_sem.at[r])

    lanes = lax.broadcasted_iota(jnp.int32, (length, length), 1)

    per = 128 // box
    lane_groups = box * box // 128

    def z_stage(r):
        for half, table in enumerate((tza, tzb)):
            skip, size, top = half * cuts[0][2], cuts[half][2], tops[half]
            cells = jnp.concatenate([lbuf[r, s * block + skip : s * block + skip + size] for s in range(groups)], axis=0)
            out = mul(table[0], cells) + mul(table[1], cells)
            to = half * tops[0]
            a_buf[to : to + top] = out[:top]
            a_buf[rows + to : rows + to + top] = out[top:]

    first_lanes = lax.broadcasted_iota(jnp.int32, (rows, 128), 1) < 64

    def lane_group(j, b_re, b_im):
        at = pl.ds(pl.multiple_of(j * 128, 128), 128)
        whole, early, late = [], [], []
        for values in (a_buf[0:rows, at], a_buf[rows : 2 * rows, at]):
            upper = values.astype(BF)
            wide = upper.astype(F32)
            lower = pltpu.roll(values - wide, 64, 1)
            whole.append(upper)
            early.append(jnp.where(first_lanes, wide, lower).astype(BF))
            late.append(jnp.where(first_lanes, lower, wide).astype(BF))
        for i in range(per):
            out = mul(jnp.concatenate((early if i < per // 2 else late) + whole, axis=1), wy_ref[i])
            for g in range(rows // 8):
                to = pl.ds(pl.multiple_of((g * box + j * per + i) * 8, 8), 8)
                b_re[to, :] = out[g * 8 : g * 8 + 8, :length]
                b_im[to, :] = out[g * 8 : g * 8 + 8, length:]

    def release(r):
        for s in range(groups - 1):
            send_all(r, s).wait_send()
        keep(r).wait()

    def forward(r, b_re, b_im, next_re, next_im):
        q = lax.rem(r, 2)

        @pl.when(r + 1 < rotations)
        def _():
            finish(r + 1)

        z_stage(jnp.minimum(r + 1, rotations - 1))

        @pl.when(r + 2 < rotations)
        def _():
            relay(r + 2)

        @pl.when(r + 3 < rotations)
        def _():
            begin(r + 3)

        @pl.when(r >= 2)
        def _():
            release(r - 2)

        def x_stage(k, spec):
            for p in range(pairs):
                pair = range(2 * p, min(2 * p + 2, channels))
                def pick(ref):
                    parts = []
                    for c in pair:
                        row = k * middle + c if c < middle else tops[0] + k * (channels - middle) + c - middle
                        parts.append(ref[pl.ds(row // 8 * (box * 8) + lax.rem(row, 8), box, stride=8), :])
                    return split(jnp.concatenate(parts, axis=1))
                re_hi, re_lo = pick(b_re)
                im_hi, im_lo = pick(b_im)
                right = jnp.concatenate([re_hi, im_hi, re_lo, im_lo, re_hi, im_hi], axis=0)
                spec[p, :, 0 : length * len(pair)] = mul(tx_ref[...], right)

        def product(k, spec, square):
            for h in range(0, length, 16):
                low, high = slice(h, h + 16), slice(length + h, length + h + 16)
                p_re = p_im = None
                for c in range(channels):
                    at = slice((c % 2) * length, (c % 2 + 1) * length)
                    s_re = spec[c // 2, low, at]
                    s_im = spec[c // 2, high, at]
                    r_re = rec[0, c, k, low]
                    r_im = rec[1, c, k, low]
                    q_re = r_re * s_re + r_im * s_im
                    q_im = r_im * s_re - r_re * s_im
                    p_re = q_re if p_re is None else p_re + q_re
                    p_im = q_im if p_im is None else p_im + q_im
                for t, (re, im) in enumerate(zip(split(p_re), split(p_im))):
                    square[t, low, 0:length] = re
                    square[t, low, length : 2 * length] = im
                    square[t, high, 0:length] = -im
                    square[t, high, length : 2 * length] = re

        def close(k, square):
            upper = square[0]
            field = mul(ti_ref[...], jnp.concatenate([upper, upper, square[1]], axis=0))
            most = jnp.max(jnp.abs(field), axis=1, keepdims=True)
            code = jnp.ceil(LEVELS * jnp.log2(jnp.maximum(most, 1e-30))) + 1.0
            factor = TOP * jnp.exp2(code * (-1.0 / LEVELS))
            qbuf[q, k] = jnp.round(field * factor).astype(jnp.int32).reshape(groups, xs, 2 * length).astype(jnp.int16)
            expo[...] = jnp.where(lanes == k, code, expo[...])

        def send(k):
            for s in range(groups - 1):
                send_plane(r, k, s).start()

        each = -(-lane_groups // (planes // 2))

        def two(m, carry):
            k = 2 * m
            x_stage(k - 1, spec_b)
            for g in range(each):
                lane_group(jnp.minimum((m - 1) * each + g, lane_groups - 1), next_re, next_im)
            product(k - 2, spec_a, square_a)
            close(jnp.maximum(k - 3, 0), square_b)
            x_stage(k, spec_a)
            product(k - 1, spec_b, square_b)
            close(k - 2, square_a)

            @pl.when(m > 1)
            def _():
                send(k - 3)

            send(k - 2)
            return carry

        x_stage(0, spec_a)
        lax.fori_loop(1, planes // 2 + 1, two, 0)
        product(planes - 1, spec_a, square_a)
        close(planes - 2, square_b)
        close(planes - 1, square_a)
        send(planes - 2)
        send(planes - 1)
        codes = expo[...].astype(jnp.int32)
        codes = jnp.concatenate([codes, codes], axis=1)
        qbuf[q, planes] = codes.reshape(groups, xs, 2 * length).astype(jnp.int16)
        send(planes)
        keep(r).start()

    for r in range(min(3, rotations)):
        begin(r)

    def widen(k, carry):
        @pl.when(k + 1 < planes)
        def _():
            fetch(k + 1).start()

        fetch(k).wait()
        for part in range(2):
            for c in range(channels):
                rec[part, c, k] = stage[lax.rem(k, 2), part, c].astype(F32)
        return carry

    lax.fori_loop(0, planes, widen, 0)
    for copy in table_copies:
        copy.wait()
    relay(0)
    finish(0)
    z_stage(0)
    if rotations > 1:
        relay(1)

    def first(j, carry):
        lane_group(j, even_re, even_im)
        return carry

    lax.fori_loop(0, lane_groups, first, 0)

    parts = xs // width

    def load_block(f, h):
        return pltpu.make_async_copy(recv_hbm.at[f, :, :, pl.ds(h * width, width)], blocks.at[h], in_sem.at[h])

    def store_block(f, h):
        return pltpu.make_async_copy(ready.at[h], early_hbm.at[f, pl.ds(h * width, width)], out_sem.at[h])

    def end(f, carry):
        for s in range(groups - 1):
            send_all(f, s).wait_recv()
        for h in range(parts):
            load_block(f, h).start()
        for h in range(parts):
            @pl.when(f > 0)
            def _():
                store_block(f - 1, h).wait()

            load_block(f, h).wait()
            end_block(
                groups, planes, length, width, terms, lambda s, k: blocks[h, s, k], ty_ref, tb_ref,
                ready.at[h], low_ref.at[f, h], h_re, h_im)
            store_block(f, h).start()
        return carry

    def rotation_pair(p, carry):
        forward(2 * p, even_re, even_im, odd_re, odd_im)
        forward(2 * p + 1, odd_re, odd_im, even_re, even_im)
        lax.fori_loop(jnp.maximum(2 * p - 2, 0), 2 * p, end, 0)
        return carry

    lax.fori_loop(0, rotations // 2, rotation_pair, 0)
    if rotations % 2:
        forward(rotations - 1, even_re, even_im, odd_re, odd_im)
    for r in range(max(rotations - 2, 0), rotations):
        release(r)
    early = 2 * (rotations // 2) - 2
    for h in range(parts):
        store_block(early - 1, h).wait()

    def drain(r, carry):
        for k in range(len(peers)):
            own_copy(r, k).wait_send()
        for k in range(len(far)):
            relay_copy(r, k).wait_send()
        @pl.when(r >= early)
        def _():
            for s in range(groups - 1):
                send_all(r, s).wait_recv()

        return carry

    lax.fori_loop(0, rotations, drain, 0)


def end_block(groups, planes, length, width, terms, read, ty_ref, tz_ref, out_ref, low_ref, h_re, h_im):
    for s in range(groups):
        code = read(s, planes).astype(jnp.int32).astype(F32)[:, :length]
        scale = jnp.exp2(code * (1.0 / LEVELS)) * (1.0 / TOP)
        parts = [read(s, k).astype(jnp.int32).astype(F32) * scale[:, k : k + 1] for k in range(planes)]
        upper, lower = split(jnp.concatenate(parts, axis=0))
        lines = mul(jnp.concatenate([upper, upper, lower], axis=1), ty_ref[...])
        at = pl.ds(s * planes * width, planes * width)
        h_re[at, :] = lines[:, :length]
        h_im[at, :] = lines[:, length:]
    if terms > groups * planes:
        rest = pl.ds(groups * planes * width, (terms - groups * planes) * width)
        h_re[rest, :] = jnp.zeros(((terms - groups * planes) * width, length), F32)
        h_im[rest, :] = jnp.zeros(((terms - groups * planes) * width, length), F32)
    for i in range(0, width, 2):
        def both(ref):
            return split(jnp.concatenate([ref[pl.ds(i + t, terms, stride=width), :] for t in range(2)], axis=1))
        re_hi, re_lo = both(h_re)
        im_hi, im_lo = both(h_im)
        right = jnp.concatenate([re_hi, im_hi, re_lo, im_lo, re_hi, im_hi], axis=0)
        field = mul(tz_ref[...], right)
        for t in range(2):
            plane = field[:, t * length : (t + 1) * length]
            low_ref[i + t : i + t + 1, :] = jnp.min(plane, axis=0, keepdims=True)
            out_ref[i + t] = plane.T


def final_kernel(
    groups, planes, length, width, terms, early, parts, steps,
    blocks_ref, early_hbm, ty_ref, tz_ref, out_hbm, low_ref, ready, h_re, h_im, hold, copy_sem, out_sem,
):
    step = pl.program_id(0) * parts + pl.program_id(1)

    def store_block(t):
        at = pl.ds(pl.multiple_of(lax.rem(t, parts) * width, width), width)
        return pltpu.make_async_copy(ready.at[lax.rem(t, 2)], out_hbm.at[early + t // parts, at], out_sem.at[lax.rem(t, 2)])

    def bring(r):
        return pltpu.make_async_copy(early_hbm.at[r], hold.at[r], copy_sem.at[0, r])

    def hand(r):
        return pltpu.make_async_copy(hold.at[r], out_hbm.at[r], copy_sem.at[1, r])

    @pl.when(step == 0)
    def _():
        for r in range(early):
            bring(r).start()

    for r in range(early):
        @pl.when(step == min(r + 1, steps - 1))
        def _():
            bring(r).wait()
            hand(r).start()

    @pl.when(step >= 2)
    def _():
        store_block(step - 2).wait()

    end_block(
        groups, planes, length, width, terms, lambda s, k: blocks_ref[0, s, k], ty_ref, tz_ref,
        ready.at[lax.rem(step, 2)], low_ref.at[0, 0], h_re, h_im)
    store_block(step).start()
    @pl.when(step == steps - 1)
    def _():
        if steps > 1:
            store_block(step - 1).wait()
        store_block(step).wait()
        for r in range(early):
            hand(r).wait()


def best_kernel(groups, rotations, early, first_ref, last_ref, out_ref, held, send_sem, recv_sem):
    me = lax.axis_index("fft")
    others = [lax.rem(me + s, groups) for s in range(1, groups)]
    barrier = pltpu.get_barrier_semaphore()
    for peer in others:
        pl.semaphore_signal(barrier, inc=1, device_id={"fft": peer}, device_id_type=pl.DeviceIdType.MESH)
    held[me, 0:early] = jnp.min(first_ref[...], axis=(1, 2))
    held[me, early:rotations] = jnp.min(last_ref[...], axis=(1, 2))
    pl.semaphore_wait(barrier, groups - 1)

    def share(s):
        return pltpu.make_async_remote_copy(
            src_ref=held.at[me], dst_ref=held.at[me], send_sem=send_sem.at[s], recv_sem=recv_sem.at[me],
            device_id={"fft": others[s]}, device_id_type=pl.DeviceIdType.MESH)

    def arrival(s):
        return pltpu.make_async_remote_copy(
            src_ref=held.at[me], dst_ref=held.at[others[s]], send_sem=send_sem.at[s], recv_sem=recv_sem.at[others[s]],
            device_id={"fft": others[s]}, device_id_type=pl.DeviceIdType.MESH)

    for s in range(groups - 1):
        share(s).start()
    for s in range(groups - 1):
        arrival(s).wait_recv()
        share(s).wait_send()
    low = jnp.min(jnp.min(held[...], axis=0), axis=1, keepdims=True)
    lane = lax.broadcasted_iota(jnp.int32, (rotations, 128), 1)
    row = lax.broadcasted_iota(jnp.int32, (rotations, 128), 0)
    out_ref[...] = jnp.sum(jnp.where(lane == row, low, 0.0), axis=0, keepdims=True)[:, :rotations]


def shards(receptor, ligand_grids, rot_index):
    groups = lax.axis_size("fft")
    channels, slab, length = receptor.shape[1], receptor.shape[2], receptor.shape[3]
    depth = ligand_grids.shape[2]
    box = depth * groups
    cells = ligand_grids.shape[3]
    rotations = rot_index.shape[0]
    xs = length // groups
    planes = slab // 2 + 1
    middle = (channels + 1) // 2
    cuts = tuple((start, stop, up((stop - start) * depth, 16)) for start, stop in ((0, middle), (middle, channels)))
    block = cuts[0][2] + cuts[1][2]
    top = up(planes * middle, 8)
    rows = up(top + planes * (channels - middle), 16)
    tops = (top, rows - top)
    freq = np.arange(length)

    t_z = []
    for (start, stop, size), top in zip(cuts, tops):
        table = np.zeros((groups, 2, top, groups, size))
        for d in range(groups):
            cz, sz = trig(d * slab + np.arange(planes), np.arange(box), length)
            for c in range(stop - start):
                at = np.arange(planes) * (stop - start) + c
                for s in range(groups):
                    span = slice(c * depth, (c + 1) * depth)
                    cut = slice(s * depth, (s + 1) * depth)
                    table[d, 0, at, s, span] = cz[:, cut]
                    table[d, 1, at, s, span] = -sz[:, cut]
        table = table.reshape(groups, 2 * top, groups * size)
        t_z.append(jnp.asarray(np.stack(halves(table), axis=1)))

    cy, sy = trig(np.arange(box), freq, length)
    per = 128 // box
    hi, lo = halves(np.concatenate([cy, -sy], axis=1)), halves(np.concatenate([sy, cy], axis=1))
    w_y = np.zeros((per, 512, 2 * length), ml_dtypes.bfloat16)
    for i in range(per):
        for part, (upper, lower) in enumerate((hi, lo)):
            for spot in (i * box, (i * box + 64) % 128):
                w_y[i, part * 128 + spot : part * 128 + spot + box] = upper
            w_y[i, 256 + part * 128 + i * box : 256 + part * 128 + (i + 1) * box] = lower
    w_y = jnp.asarray(w_y)

    t_x = np.block([[cy.T, sy.T], [-sy.T, cy.T]])
    hi, lo = halves(t_x)
    t_x = jnp.asarray(np.concatenate([hi, hi, lo], axis=1))

    cf, sf = trig(freq, freq, length)
    hi, lo = halves(np.concatenate([cf, sf], axis=1))
    t_i = jnp.asarray(np.concatenate([hi, lo, hi], axis=1))

    terms = up(groups * planes, 16)
    kz = np.zeros(terms, np.int64)
    weight = np.zeros(terms)
    for d in range(groups):
        for k in range(planes):
            f = d * slab + k
            kz[d * planes + k] = f
            if d < groups // 2:
                used = k < slab // 2
            else:
                used = k > 0 or f == length // 2
            weight[d * planes + k] = 0.0 if not used else 1.0 if f in (0, length // 2) else 2.0
    cb, sb = trig(freq, kz, length)
    hi, lo = halves(np.concatenate([cb * weight, -sb * weight], axis=1))
    t_b = jnp.asarray(np.concatenate([hi, hi, lo], axis=1))
    hi, lo = halves(np.block([[cf, sf], [-sf, cf]]) / float(length) ** 3)
    t_w = jnp.asarray(np.concatenate([hi, lo, hi], axis=0))

    any_space = pl.BlockSpec(memory_space=pl.ANY)
    vmem = pl.BlockSpec(memory_space=pltpu.VMEM)
    own = pl.pallas_call(
        functools.partial(pick_kernel, cuts),
        in_specs=[pl.BlockSpec(memory_space=pltpu.SMEM), any_space],
        out_specs=vmem,
        out_shape=jax.ShapeDtypeStruct((rotations, block, cells), BF),
        scratch_shapes=[
            pltpu.VMEM((rotations, channels, depth, cells), BF),
            pltpu.SemaphoreType.DMA((rotations,)),
        ],
    )(rot_index, ligand_grids)

    width = min(16, xs)
    parts = xs // width
    early = 2 * (rotations // 2) - 2
    late = rotations - early
    sent, early_scores, early_lows = pl.pallas_call(
        functools.partial(main_kernel, channels, planes, box, groups, rotations, length, cuts, tops, width, terms),
        in_specs=[any_space] * 4 + [vmem] * 5,
        out_specs=[any_space, any_space, vmem],
        out_shape=[
            jax.ShapeDtypeStruct((rotations, groups, planes + 1, xs, 2 * length), jnp.int16),
            jax.ShapeDtypeStruct((early, xs, length, length), F32),
            jax.ShapeDtypeStruct((early, parts, width, length), F32),
        ],
        scratch_shapes=[
            pltpu.VMEM((2, channels, planes, length, length), F32),
            pltpu.VMEM((2, 2, channels, length, length), BF),
            pltpu.VMEM((rotations, groups * block, cells), BF),
            pltpu.VMEM(t_z[0].shape[1:], BF),
            pltpu.VMEM(t_z[1].shape[1:], BF),
            pltpu.VMEM((2 * rows, cells), F32),
            pltpu.VMEM((rows * box, length), F32),
            pltpu.VMEM((rows * box, length), F32),
            pltpu.VMEM((rows * box, length), F32),
            pltpu.VMEM((rows * box, length), F32),
            pltpu.VMEM((-(-channels // 2), 2 * length, 2 * length), F32),
            pltpu.VMEM((-(-channels // 2), 2 * length, 2 * length), F32),
            pltpu.VMEM((2, 2 * length, 2 * length), BF),
            pltpu.VMEM((2, 2 * length, 2 * length), BF),
            pltpu.VMEM((length, length), F32),
            pltpu.VMEM((2, planes + 1, groups, xs, 2 * length), jnp.int16),
            pltpu.VMEM((parts, groups, planes + 1, width, 2 * length), jnp.int16),
            pltpu.VMEM((parts, width, length, length), F32),
            pltpu.VMEM((terms * width, length), F32),
            pltpu.VMEM((terms * width, length), F32),
            pltpu.SemaphoreType.DMA((4,)),
            pltpu.SemaphoreType.DMA((rotations,)),
            pltpu.SemaphoreType.DMA((rotations, groups)),
            pltpu.SemaphoreType.DMA((rotations, groups)),
            pltpu.SemaphoreType.DMA((rotations, groups)),
            pltpu.SemaphoreType.DMA((rotations, groups)),
            pltpu.SemaphoreType.DMA((rotations,)),
            pltpu.SemaphoreType.DMA((parts,)),
            pltpu.SemaphoreType.DMA((parts,)),
        ],
        compiler_params=pltpu.CompilerParams(
            collective_id=0, has_side_effects=True, vmem_limit_bytes=60 * 2**20),
        cost_estimate=pl.CostEstimate(flops=rotations * 6 * 10**9, bytes_accessed=30_000_000, transcendentals=0),
    )(receptor, own, *t_z, w_y, t_x, t_i, t_w, t_b)

    scores, late_lows = pl.pallas_call(
        functools.partial(final_kernel, groups, planes, length, width, terms, early, parts, late * parts),
        grid=(late, parts),
        in_specs=[
            pl.BlockSpec((1, groups, planes + 1, width, 2 * length), lambda r, x: (early + r, 0, 0, x, 0)),
            any_space,
            pl.BlockSpec(t_w.shape, lambda r, x: (0, 0)),
            pl.BlockSpec(t_b.shape, lambda r, x: (0, 0)),
        ],
        out_specs=[any_space, pl.BlockSpec((1, 1, width, length), lambda r, x: (r, x, 0, 0))],
        out_shape=[
            jax.ShapeDtypeStruct((rotations, xs, length, length), F32),
            jax.ShapeDtypeStruct((late, parts, width, length), F32),
        ],
        scratch_shapes=[
            pltpu.VMEM((2, width, length, length), F32),
            pltpu.VMEM((terms * width, length), F32),
            pltpu.VMEM((terms * width, length), F32),
            pltpu.VMEM((early, xs, length, length), F32),
            pltpu.SemaphoreType.DMA((2, early)),
            pltpu.SemaphoreType.DMA((2,)),
        ],
        compiler_params=pltpu.CompilerParams(vmem_limit_bytes=60 * 2**20),
        cost_estimate=pl.CostEstimate(flops=late * 10**9, bytes_accessed=20_000_000, transcendentals=0),
    )(sent, early_scores, t_w, t_b)
    best = pl.pallas_call(
        functools.partial(best_kernel, groups, rotations, early),
        in_specs=[vmem, vmem],
        out_specs=vmem,
        out_shape=jax.ShapeDtypeStruct((1, rotations), F32),
        scratch_shapes=[
            pltpu.VMEM((groups, rotations, length), F32),
            pltpu.SemaphoreType.DMA((groups,)),
            pltpu.SemaphoreType.DMA((groups,)),
        ],
        compiler_params=pltpu.CompilerParams(collective_id=1, has_side_effects=True),
    )(early_lows, late_lows)
    return scores, best.reshape(rotations)


def solution(mesh):
    placed = (P(None, None, "fft", None, None), P(None, None, "fft", None), P("rot"))
    return jax.shard_map(
        shards,
        mesh=mesh,
        in_specs=placed,
        out_specs=(P("rot", "fft", None, None), P("rot")),
        check_vma=False,
    )
```

```python
import functools
import math

import jax
import jax.numpy as jnp
import ml_dtypes
import numpy as np
from jax import lax
from jax.experimental import pallas as pl
from jax.experimental.pallas import tpu as pltpu
from jax.sharding import PartitionSpec as P

BF = jnp.bfloat16
F32 = jnp.float32
TOP = 32767.0
LEVELS = 256.0


def halves(table):
    upper = table.astype(np.float32).astype(ml_dtypes.bfloat16)
    lower = (table - upper.astype(np.float64)).astype(np.float32)
    return upper, lower.astype(ml_dtypes.bfloat16)


def trig(rows, cols, length):
    angle = (np.outer(rows, cols) % length) * (2.0 * math.pi / length)
    return np.cos(angle), np.sin(angle)


def split(values):
    upper = values.astype(BF)
    return upper, (values - upper.astype(F32)).astype(BF)


def mul(left, right):
    return jnp.dot(left, right, preferred_element_type=F32)


def mul_t(left, right):
    return lax.dot_general(left, right, (((1,), (1,)), ((), ())), preferred_element_type=F32)


def up(value, step):
    return -(-value // step) * step


def pick_kernel(cuts, index_ref, table_hbm, out_ref, held, sems):
    rotations, depth, cells = held.shape[0], held.shape[2], held.shape[3]

    def fetch(r):
        return pltpu.make_async_copy(table_hbm.at[index_ref[r]], held.at[r], sems.at[r])

    for r in range(rotations):
        fetch(r).start()
    for r in range(rotations):
        fetch(r).wait()
        parts = []
        for start, stop, size in cuts:
            parts += [held[r, c].astype(F32) for c in range(start, stop)]
            if size > (stop - start) * depth:
                parts.append(jnp.zeros((size - (stop - start) * depth, cells), F32))
        out_ref[r] = jnp.concatenate(parts, axis=0).astype(BF)


def main_kernel(
    channels, planes, box, groups, rotations, length, cuts, tops, width, terms,
    rec_hbm, own_hbm, tza_hbm, tzb_hbm, wy_ref, tx_ref, ti_ref, ty_ref, tb_ref, recv_hbm, early_hbm, low_ref,
    rec, stage, lbuf, tza, tzb, a_buf, even_re, even_im, odd_re, odd_im, spec_a, spec_b, square_a, square_b, expo, qbuf, blocks, ready, h_re, h_im,
    load_sem, own_sem, gsend, grecv, xsend, xrecv, self_sem, in_sem, out_sem,
):
    me = lax.axis_index("fft")
    block = cuts[0][2] + cuts[1][2]
    rows = tops[0] + tops[1]
    middle = cuts[1][0]
    xs = length // groups
    sib = me + 1 - 2 * lax.rem(me, 2)
    far = [lax.rem(me + 2 * m, groups) for m in range(1, groups // 2)]
    peers = [sib] + far
    others = [lax.rem(me + s, groups) for s in range(1, groups)]
    pairs = -(-channels // 2)

    def fetch(k):
        slot_at = lax.rem(k, 2)
        return pltpu.make_async_copy(rec_hbm.at[:, :, k], stage.at[slot_at], load_sem.at[slot_at])

    fetch(0).start()
    table_copies = [
        pltpu.make_async_copy(tza_hbm.at[me], tza, load_sem.at[2]),
        pltpu.make_async_copy(tzb_hbm.at[me], tzb, load_sem.at[3]),
    ]
    for copy in table_copies:
        copy.start()

    barrier = pltpu.get_barrier_semaphore()
    for peer in others:
        pl.semaphore_signal(barrier, inc=1, device_id={"fft": peer}, device_id_type=pl.DeviceIdType.MESH)
    pl.semaphore_wait(barrier, groups - 1)

    def slot(r, source):
        return lbuf.at[r, pl.ds(pl.multiple_of(source * block, block), block)]

    def own_copy(r, k):
        return pltpu.make_async_remote_copy(
            src_ref=own_hbm.at[r], dst_ref=slot(r, me), send_sem=gsend.at[r, k], recv_sem=grecv.at[r, me],
            device_id={"fft": peers[k]}, device_id_type=pl.DeviceIdType.MESH)

    def relay_copy(r, k):
        return pltpu.make_async_remote_copy(
            src_ref=slot(r, far[k]), dst_ref=slot(r, far[k]), send_sem=gsend.at[r, len(peers) + k],
            recv_sem=grecv.at[r, far[k]], device_id={"fft": sib}, device_id_type=pl.DeviceIdType.MESH)

    def arrival(r, source):
        return pltpu.make_async_remote_copy(
            src_ref=own_hbm.at[r], dst_ref=slot(r, source), send_sem=gsend.at[r, 0], recv_sem=grecv.at[r, source],
            device_id={"fft": sib}, device_id_type=pl.DeviceIdType.MESH)

    def local(r):
        return pltpu.make_async_copy(own_hbm.at[r], slot(r, me), own_sem.at[r])

    def begin(r):
        for k in range(len(peers)):
            own_copy(r, k).start()
        local(r).start()

    def relay(r):
        for k in range(len(far)):
            arrival(r, far[k]).wait_recv()
            relay_copy(r, k).start()

    def finish(r):
        arrival(r, sib).wait_recv()
        for m in range(1, groups // 2):
            arrival(r, lax.rem(sib + 2 * m, groups)).wait_recv()
        local(r).wait()

    def send_plane(r, k, s):
        peer = others[s]
        return pltpu.make_async_remote_copy(
            src_ref=qbuf.at[lax.rem(r, 2), k, peer], dst_ref=recv_hbm.at[r, me, k],
            send_sem=xsend.at[r, s], recv_sem=xrecv.at[r, me],
            device_id={"fft": peer}, device_id_type=pl.DeviceIdType.MESH)

    def send_all(r, s):
        peer = others[s]
        return pltpu.make_async_remote_copy(
            src_ref=qbuf.at[lax.rem(r, 2), :, peer], dst_ref=recv_hbm.at[r, peer],
            send_sem=xsend.at[r, s], recv_sem=xrecv.at[r, peer],
            device_id={"fft": peer}, device_id_type=pl.DeviceIdType.MESH)

    def keep(r):
        return pltpu.make_async_copy(
            qbuf.at[lax.rem(r, 2), :, me], recv_hbm.at[r, me], self_sem.at[r])

    lanes = lax.broadcasted_iota(jnp.int32, (length, length), 1)

    per = 128 // box
    lane_groups = box * box // 128

    def z_stage(r):
        for half, table in enumerate((tza, tzb)):
            skip, size, top = half * cuts[0][2], cuts[half][2], tops[half]
            cells = jnp.concatenate([lbuf[r, s * block + skip : s * block + skip + size] for s in range(groups)], axis=0)
            out = mul(table[0], cells) + mul(table[1], cells)
            to = half * tops[0]
            a_buf[to : to + top] = out[:top]
            a_buf[rows + to : rows + to + top] = out[top:]

    first_lanes = lax.broadcasted_iota(jnp.int32, (rows, 128), 1) < 64

    def lane_group(j, b_re, b_im):
        at = pl.ds(pl.multiple_of(j * 128, 128), 128)
        whole, early, late = [], [], []
        for values in (a_buf[0:rows, at], a_buf[rows : 2 * rows, at]):
            upper = values.astype(BF)
            wide = upper.astype(F32)
            lower = pltpu.roll(values - wide, 64, 1)
            whole.append(upper)
            early.append(jnp.where(first_lanes, wide, lower).astype(BF))
            late.append(jnp.where(first_lanes, lower, wide).astype(BF))
        for i in range(per):
            out = mul(jnp.concatenate((early if i < per // 2 else late) + whole, axis=1), wy_ref[i])
            for g in range(rows // 8):
                to = pl.ds(pl.multiple_of((g * box + j * per + i) * 8, 8), 8)
                b_re[to, :] = out[g * 8 : g * 8 + 8, :length]
                b_im[to, :] = out[g * 8 : g * 8 + 8, length:]

    def release(r):
        for s in range(groups - 1):
            send_all(r, s).wait_send()
        keep(r).wait()

    def forward(r, b_re, b_im, next_re, next_im):
        q = lax.rem(r, 2)

        @pl.when(r + 1 < rotations)
        def _():
            finish(r + 1)

        z_stage(jnp.minimum(r + 1, rotations - 1))

        @pl.when(r + 2 < rotations)
        def _():
            relay(r + 2)

        @pl.when(r + 3 < rotations)
        def _():
            begin(r + 3)

        @pl.when(r >= 2)
        def _():
            release(r - 2)

        def x_stage(k, spec):
            for p in range(pairs):
                pair = range(2 * p, min(2 * p + 2, channels))
                def pick(ref):
                    parts = []
                    for c in pair:
                        row = k * middle + c if c < middle else tops[0] + k * (channels - middle) + c - middle
                        parts.append(ref[pl.ds(row // 8 * (box * 8) + lax.rem(row, 8), box, stride=8), :])
                    return split(jnp.concatenate(parts, axis=1))
                re_hi, re_lo = pick(b_re)
                im_hi, im_lo = pick(b_im)
                right = jnp.concatenate([re_hi, im_hi, re_lo, im_lo, re_hi, im_hi], axis=0)
                spec[p, :, 0 : length * len(pair)] = mul(tx_ref[...], right)

        def product(k, spec, square):
            for h in range(0, length, 16):
                low, high = slice(h, h + 16), slice(length + h, length + h + 16)
                p_re = p_im = None
                for c in range(channels):
                    at = slice((c % 2) * length, (c % 2 + 1) * length)
                    s_re = spec[c // 2, low, at]
                    s_im = spec[c // 2, high, at]
                    r_re = rec[0, c, k, low]
                    r_im = rec[1, c, k, low]
                    q_re = r_re * s_re + r_im * s_im
                    q_im = r_im * s_re - r_re * s_im
                    p_re = q_re if p_re is None else p_re + q_re
                    p_im = q_im if p_im is None else p_im + q_im
                for t, (re, im) in enumerate(zip(split(p_re), split(p_im))):
                    square[t, low, 0:length] = re
                    square[t, low, length : 2 * length] = im
                    square[t, high, 0:length] = -im
                    square[t, high, length : 2 * length] = re

        def close(k, square):
            upper = square[0]
            field = mul(ti_ref[...], jnp.concatenate([upper, upper, square[1]], axis=0))
            most = jnp.max(jnp.abs(field), axis=1, keepdims=True)
            code = jnp.ceil(LEVELS * jnp.log2(jnp.maximum(most, 1e-30))) + 1.0
            factor = TOP * jnp.exp2(code * (-1.0 / LEVELS))
            qbuf[q, k] = jnp.round(field * factor).astype(jnp.int32).reshape(groups, xs, 2 * length).astype(jnp.int16)
            expo[...] = jnp.where(lanes == k, code, expo[...])

        def send(k):
            for s in range(groups - 1):
                send_plane(r, k, s).start()

        each = -(-lane_groups // (planes // 2))

        def two(m, carry):
            k = 2 * m
            x_stage(k - 1, spec_b)
            for g in range(each):
                lane_group(jnp.minimum((m - 1) * each + g, lane_groups - 1), next_re, next_im)
            product(k - 2, spec_a, square_a)
            close(jnp.maximum(k - 3, 0), square_b)
            x_stage(k, spec_a)
            product(k - 1, spec_b, square_b)
            close(k - 2, square_a)

            @pl.when(m > 1)
            def _():
                send(k - 3)

            send(k - 2)
            return carry

        x_stage(0, spec_a)
        lax.fori_loop(1, planes // 2 + 1, two, 0)
        product(planes - 1, spec_a, square_a)
        close(planes - 2, square_b)
        close(planes - 1, square_a)
        send(planes - 2)
        send(planes - 1)
        codes = expo[...].astype(jnp.int32)
        codes = jnp.concatenate([codes, codes], axis=1)
        qbuf[q, planes] = codes.reshape(groups, xs, 2 * length).astype(jnp.int16)
        send(planes)
        keep(r).start()

    for r in range(min(3, rotations)):
        begin(r)

    def widen(k, carry):
        @pl.when(k + 1 < planes)
        def _():
            fetch(k + 1).start()

        fetch(k).wait()
        for part in range(2):
            for c in range(channels):
                rec[part, c, k] = stage[lax.rem(k, 2), part, c].astype(F32)
        return carry

    lax.fori_loop(0, planes, widen, 0)
    for copy in table_copies:
        copy.wait()
    relay(0)
    finish(0)
    z_stage(0)
    if rotations > 1:
        relay(1)

    def first(j, carry):
        lane_group(j, even_re, even_im)
        return carry

    lax.fori_loop(0, lane_groups, first, 0)

    parts = xs // width
    early = 2 * (rotations // 2) - 3

    def load_block(f, h):
        return pltpu.make_async_copy(recv_hbm.at[f, :, :, pl.ds(h * width, width)], blocks.at[h], in_sem.at[h])

    def store_block(f, h):
        return pltpu.make_async_copy(ready.at[h], early_hbm.at[f, pl.ds(h * width, width)], out_sem.at[h])

    def end(f, carry):
        for s in range(groups - 1):
            send_all(f, s).wait_recv()
        for h in range(parts):
            load_block(f, h).start()
        for h in range(parts):
            @pl.when(f > 0)
            def _():
                store_block(f - 1, h).wait()

            load_block(f, h).wait()
            end_block(
                groups, planes, length, width, terms, lambda s, k: blocks[h, s, k], ty_ref, tb_ref,
                ready.at[h], low_ref.at[f, h], h_re, h_im)
            store_block(f, h).start()
        return carry

    def rotation_pair(p, carry):
        forward(2 * p, even_re, even_im, odd_re, odd_im)
        forward(2 * p + 1, odd_re, odd_im, even_re, even_im)
        lax.fori_loop(jnp.maximum(2 * p - 2, 0), jnp.minimum(2 * p, early), end, 0)
        return carry

    lax.fori_loop(0, rotations // 2, rotation_pair, 0)
    if rotations % 2:
        forward(rotations - 1, even_re, even_im, odd_re, odd_im)
    for r in range(max(rotations - 2, 0), rotations):
        release(r)
    for h in range(parts):
        store_block(early - 1, h).wait()

    def drain(r, carry):
        for k in range(len(peers)):
            own_copy(r, k).wait_send()
        for k in range(len(far)):
            relay_copy(r, k).wait_send()
        @pl.when(r >= early)
        def _():
            for s in range(groups - 1):
                send_all(r, s).wait_recv()

        return carry

    lax.fori_loop(0, rotations, drain, 0)


def end_block(groups, planes, length, width, terms, read, ty_ref, tz_ref, out_ref, low_ref, h_re, h_im):
    for s in range(groups):
        code = read(s, planes).astype(jnp.int32).astype(F32)[:, :length]
        scale = jnp.exp2(code * (1.0 / LEVELS)) * (1.0 / TOP)
        parts = [read(s, k).astype(jnp.int32).astype(F32) * scale[:, k : k + 1] for k in range(planes)]
        upper, lower = split(jnp.concatenate(parts, axis=0))
        lines = mul(jnp.concatenate([upper, upper, lower], axis=1), ty_ref[...])
        at = pl.ds(s * planes * width, planes * width)
        h_re[at, :] = lines[:, :length]
        h_im[at, :] = lines[:, length:]
    if terms > groups * planes:
        rest = pl.ds(groups * planes * width, (terms - groups * planes) * width)
        h_re[rest, :] = jnp.zeros(((terms - groups * planes) * width, length), F32)
        h_im[rest, :] = jnp.zeros(((terms - groups * planes) * width, length), F32)
    for i in range(0, width, 2):
        def both(ref):
            return split(jnp.concatenate([ref[pl.ds(i + t, terms, stride=width), :] for t in range(2)], axis=1))
        re_hi, re_lo = both(h_re)
        im_hi, im_lo = both(h_im)
        right = jnp.concatenate([re_hi, im_hi, re_lo, im_lo, re_hi, im_hi], axis=0)
        field = mul(tz_ref[...], right)
        for t in range(2):
            plane = field[:, t * length : (t + 1) * length]
            low_ref[i + t : i + t + 1, :] = jnp.min(plane, axis=0, keepdims=True)
            out_ref[i + t] = plane.T


def final_kernel(
    groups, planes, length, width, terms, early, parts, steps,
    blocks_ref, early_hbm, ty_ref, tz_ref, out_hbm, low_ref, ready, h_re, h_im, hold, copy_sem, out_sem,
):
    step = pl.program_id(0) * parts + pl.program_id(1)

    def store_block(t):
        at = pl.ds(pl.multiple_of(lax.rem(t, parts) * width, width), width)
        return pltpu.make_async_copy(ready.at[lax.rem(t, 2)], out_hbm.at[early + t // parts, at], out_sem.at[lax.rem(t, 2)])

    def bring(r):
        return pltpu.make_async_copy(early_hbm.at[r], hold.at[r], copy_sem.at[0, r])

    def hand(r):
        return pltpu.make_async_copy(hold.at[r], out_hbm.at[r], copy_sem.at[1, r])

    @pl.when(step == 0)
    def _():
        for r in range(early):
            bring(r).start()

    for r in range(early):
        @pl.when(step == min(r + 1, steps - 1))
        def _():
            bring(r).wait()
            hand(r).start()

    @pl.when(step >= 2)
    def _():
        store_block(step - 2).wait()

    end_block(
        groups, planes, length, width, terms, lambda s, k: blocks_ref[0, s, k], ty_ref, tz_ref,
        ready.at[lax.rem(step, 2)], low_ref.at[0, 0], h_re, h_im)
    store_block(step).start()
    @pl.when(step == steps - 1)
    def _():
        if steps > 1:
            store_block(step - 1).wait()
        store_block(step).wait()
        for r in range(early):
            hand(r).wait()


def best_kernel(groups, rotations, early, first_ref, last_ref, out_ref, held, send_sem, recv_sem):
    me = lax.axis_index("fft")
    others = [lax.rem(me + s, groups) for s in range(1, groups)]
    barrier = pltpu.get_barrier_semaphore()
    for peer in others:
        pl.semaphore_signal(barrier, inc=1, device_id={"fft": peer}, device_id_type=pl.DeviceIdType.MESH)
    held[me, 0:early] = jnp.min(first_ref[...], axis=(1, 2))
    held[me, early:rotations] = jnp.min(last_ref[...], axis=(1, 2))
    pl.semaphore_wait(barrier, groups - 1)

    def share(s):
        return pltpu.make_async_remote_copy(
            src_ref=held.at[me], dst_ref=held.at[me], send_sem=send_sem.at[s], recv_sem=recv_sem.at[me],
            device_id={"fft": others[s]}, device_id_type=pl.DeviceIdType.MESH)

    def arrival(s):
        return pltpu.make_async_remote_copy(
            src_ref=held.at[me], dst_ref=held.at[others[s]], send_sem=send_sem.at[s], recv_sem=recv_sem.at[others[s]],
            device_id={"fft": others[s]}, device_id_type=pl.DeviceIdType.MESH)

    for s in range(groups - 1):
        share(s).start()
    for s in range(groups - 1):
        arrival(s).wait_recv()
        share(s).wait_send()
    low = jnp.min(jnp.min(held[...], axis=0), axis=1, keepdims=True)
    lane = lax.broadcasted_iota(jnp.int32, (rotations, 128), 1)
    row = lax.broadcasted_iota(jnp.int32, (rotations, 128), 0)
    out_ref[...] = jnp.sum(jnp.where(lane == row, low, 0.0), axis=0, keepdims=True)[:, :rotations]


def shards(receptor, ligand_grids, rot_index):
    groups = lax.axis_size("fft")
    channels, slab, length = receptor.shape[1], receptor.shape[2], receptor.shape[3]
    depth = ligand_grids.shape[2]
    box = depth * groups
    cells = ligand_grids.shape[3]
    rotations = rot_index.shape[0]
    xs = length // groups
    planes = slab // 2 + 1
    middle = (channels + 1) // 2
    cuts = tuple((start, stop, up((stop - start) * depth, 16)) for start, stop in ((0, middle), (middle, channels)))
    block = cuts[0][2] + cuts[1][2]
    top = up(planes * middle, 8)
    rows = up(top + planes * (channels - middle), 16)
    tops = (top, rows - top)
    freq = np.arange(length)

    t_z = []
    for (start, stop, size), top in zip(cuts, tops):
        table = np.zeros((groups, 2, top, groups, size))
        for d in range(groups):
            cz, sz = trig(d * slab + np.arange(planes), np.arange(box), length)
            for c in range(stop - start):
                at = np.arange(planes) * (stop - start) + c
                for s in range(groups):
                    span = slice(c * depth, (c + 1) * depth)
                    cut = slice(s * depth, (s + 1) * depth)
                    table[d, 0, at, s, span] = cz[:, cut]
                    table[d, 1, at, s, span] = -sz[:, cut]
        table = table.reshape(groups, 2 * top, groups * size)
        t_z.append(jnp.asarray(np.stack(halves(table), axis=1)))

    cy, sy = trig(np.arange(box), freq, length)
    per = 128 // box
    hi, lo = halves(np.concatenate([cy, -sy], axis=1)), halves(np.concatenate([sy, cy], axis=1))
    w_y = np.zeros((per, 512, 2 * length), ml_dtypes.bfloat16)
    for i in range(per):
        for part, (upper, lower) in enumerate((hi, lo)):
            for spot in (i * box, (i * box + 64) % 128):
                w_y[i, part * 128 + spot : part * 128 + spot + box] = upper
            w_y[i, 256 + part * 128 + i * box : 256 + part * 128 + (i + 1) * box] = lower
    w_y = jnp.asarray(w_y)

    t_x = np.block([[cy.T, sy.T], [-sy.T, cy.T]])
    hi, lo = halves(t_x)
    t_x = jnp.asarray(np.concatenate([hi, hi, lo], axis=1))

    cf, sf = trig(freq, freq, length)
    hi, lo = halves(np.concatenate([cf, sf], axis=1))
    t_i = jnp.asarray(np.concatenate([hi, lo, hi], axis=1))

    terms = up(groups * planes, 16)
    kz = np.zeros(terms, np.int64)
    weight = np.zeros(terms)
    for d in range(groups):
        for k in range(planes):
            f = d * slab + k
            kz[d * planes + k] = f
            if d < groups // 2:
                used = k < slab // 2
            else:
                used = k > 0 or f == length // 2
            weight[d * planes + k] = 0.0 if not used else 1.0 if f in (0, length // 2) else 2.0
    cb, sb = trig(freq, kz, length)
    hi, lo = halves(np.concatenate([cb * weight, -sb * weight], axis=1))
    t_b = jnp.asarray(np.concatenate([hi, hi, lo], axis=1))
    hi, lo = halves(np.block([[cf, sf], [-sf, cf]]) / float(length) ** 3)
    t_w = jnp.asarray(np.concatenate([hi, lo, hi], axis=0))

    any_space = pl.BlockSpec(memory_space=pl.ANY)
    vmem = pl.BlockSpec(memory_space=pltpu.VMEM)
    own = pl.pallas_call(
        functools.partial(pick_kernel, cuts),
        in_specs=[pl.BlockSpec(memory_space=pltpu.SMEM), any_space],
        out_specs=vmem,
        out_shape=jax.ShapeDtypeStruct((rotations, block, cells), BF),
        scratch_shapes=[
            pltpu.VMEM((rotations, channels, depth, cells), BF),
            pltpu.SemaphoreType.DMA((rotations,)),
        ],
    )(rot_index, ligand_grids)

    width = min(16, xs)
    parts = xs // width
    early = 2 * (rotations // 2) - 3
    late = rotations - early
    sent, early_scores, early_lows = pl.pallas_call(
        functools.partial(main_kernel, channels, planes, box, groups, rotations, length, cuts, tops, width, terms),
        in_specs=[any_space] * 4 + [vmem] * 5,
        out_specs=[any_space, any_space, vmem],
        out_shape=[
            jax.ShapeDtypeStruct((rotations, groups, planes + 1, xs, 2 * length), jnp.int16),
            jax.ShapeDtypeStruct((early, xs, length, length), F32),
            jax.ShapeDtypeStruct((early, parts, width, length), F32),
        ],
        scratch_shapes=[
            pltpu.VMEM((2, channels, planes, length, length), F32),
            pltpu.VMEM((2, 2, channels, length, length), BF),
            pltpu.VMEM((rotations, groups * block, cells), BF),
            pltpu.VMEM(t_z[0].shape[1:], BF),
            pltpu.VMEM(t_z[1].shape[1:], BF),
            pltpu.VMEM((2 * rows, cells), F32),
            pltpu.VMEM((rows * box, length), F32),
            pltpu.VMEM((rows * box, length), F32),
            pltpu.VMEM((rows * box, length), F32),
            pltpu.VMEM((rows * box, length), F32),
            pltpu.VMEM((-(-channels // 2), 2 * length, 2 * length), F32),
            pltpu.VMEM((-(-channels // 2), 2 * length, 2 * length), F32),
            pltpu.VMEM((2, 2 * length, 2 * length), BF),
            pltpu.VMEM((2, 2 * length, 2 * length), BF),
            pltpu.VMEM((length, length), F32),
            pltpu.VMEM((2, planes + 1, groups, xs, 2 * length), jnp.int16),
            pltpu.VMEM((parts, groups, planes + 1, width, 2 * length), jnp.int16),
            pltpu.VMEM((parts, width, length, length), F32),
            pltpu.VMEM((terms * width, length), F32),
            pltpu.VMEM((terms * width, length), F32),
            pltpu.SemaphoreType.DMA((4,)),
            pltpu.SemaphoreType.DMA((rotations,)),
            pltpu.SemaphoreType.DMA((rotations, groups)),
            pltpu.SemaphoreType.DMA((rotations, groups)),
            pltpu.SemaphoreType.DMA((rotations, groups)),
            pltpu.SemaphoreType.DMA((rotations, groups)),
            pltpu.SemaphoreType.DMA((rotations,)),
            pltpu.SemaphoreType.DMA((parts,)),
            pltpu.SemaphoreType.DMA((parts,)),
        ],
        compiler_params=pltpu.CompilerParams(
            collective_id=0, has_side_effects=True, vmem_limit_bytes=60 * 2**20),
        cost_estimate=pl.CostEstimate(flops=rotations * 6 * 10**9, bytes_accessed=30_000_000, transcendentals=0),
    )(receptor, own, *t_z, w_y, t_x, t_i, t_w, t_b)

    scores, late_lows = pl.pallas_call(
        functools.partial(final_kernel, groups, planes, length, width, terms, early, parts, late * parts),
        grid=(late, parts),
        in_specs=[
            pl.BlockSpec((1, groups, planes + 1, width, 2 * length), lambda r, x: (early + r, 0, 0, x, 0)),
            any_space,
            pl.BlockSpec(t_w.shape, lambda r, x: (0, 0)),
            pl.BlockSpec(t_b.shape, lambda r, x: (0, 0)),
        ],
        out_specs=[any_space, pl.BlockSpec((1, 1, width, length), lambda r, x: (r, x, 0, 0))],
        out_shape=[
            jax.ShapeDtypeStruct((rotations, xs, length, length), F32),
            jax.ShapeDtypeStruct((late, parts, width, length), F32),
        ],
        scratch_shapes=[
            pltpu.VMEM((2, width, length, length), F32),
            pltpu.VMEM((terms * width, length), F32),
            pltpu.VMEM((terms * width, length), F32),
            pltpu.VMEM((early, xs, length, length), F32),
            pltpu.SemaphoreType.DMA((2, early)),
            pltpu.SemaphoreType.DMA((2,)),
        ],
        compiler_params=pltpu.CompilerParams(vmem_limit_bytes=60 * 2**20),
        cost_estimate=pl.CostEstimate(flops=late * 10**9, bytes_accessed=20_000_000, transcendentals=0),
    )(sent, early_scores, t_w, t_b)
    best = pl.pallas_call(
        functools.partial(best_kernel, groups, rotations, early),
        in_specs=[vmem, vmem],
        out_specs=vmem,
        out_shape=jax.ShapeDtypeStruct((1, rotations), F32),
        scratch_shapes=[
            pltpu.VMEM((groups, rotations, length), F32),
            pltpu.SemaphoreType.DMA((groups,)),
            pltpu.SemaphoreType.DMA((groups,)),
        ],
        compiler_params=pltpu.CompilerParams(collective_id=1, has_side_effects=True),
    )(early_lows, late_lows)
    return scores, best.reshape(rotations)


def solution(mesh):
    placed = (P(None, None, "fft", None, None), P(None, None, "fft", None), P("rot"))
    return jax.shard_map(
        shards,
        mesh=mesh,
        in_specs=placed,
        out_specs=(P("rot", "fft", None, None), P("rot")),
        check_vma=False,
    )
```
